128 devices in a mesh: group: 4 (over x_hi, core), tensor: 32 (over x_lo, y, z).
Axes of the slice: x: 4 (x_hi: 2, x_lo: 2; x = x_hi * 2 + x_lo), y: 4, z: 4, core: 2. Of those that a mesh axis runs over, the one named last changes fastest.
Arguments:
- tokens: bfloat16 [4096, 4096], P(('group', 'tensor')), may hold values from -6 to 6
- expert_norm_gain: float32 [4096], replicated, may hold values from 0.1 to 1.9
- routing: int32 [4096, 4], P('group'), may hold values from 0 to 15, all different within a row; in each aligned block of 32 rows (0 to 31, 32 to 63, ...) at most 16 rows name the same one
- chosen_expert_weights: float32 [4096, 4], P('group'), may hold values from 0.05 to 1
- resident_gate_weight: bfloat16 [4096, 24576], P(None, 'tensor'), may hold values from -0.09375 to 0.09375
- resident_up_weight: bfloat16 [4096, 24576], P(None, 'tensor'), may hold values from -0.09375 to 0.09375
- resident_down_weight: bfloat16 [24576, 4096], P('tensor'), may hold values from -0.15625 to 0.15625
- adapter_input_left: bfloat16 [2, 4096, 1024], P(None, 'group', 'tensor'), may hold values from -0.09375 to 0.09375
- adapter_input_right: bfloat16 [2, 64, 24576], P(None, 'group', 'tensor'), may hold values from -0.75 to 0.75
- adapter_output_left: bfloat16 [24576, 64], P('tensor', 'group'), may hold values from -0.15625 to 0.15625
- adapter_output_right: bfloat16 [64, 65536], P('group', 'tensor'), may hold values from -0.75 to 0.75
Outputs:
- mixed: bfloat16 [4096, 4096], P(('group', 'tensor'))
The draws below stay inside these ranges and needn't reach their ends.
Inputs may be any that keep to these rules, and one draw needn't show every extreme that they name: `routing`: each row names 4 different experts. Within each aligned block of 32 rows (the rows of one device) no expert is named by more than 16 rows, a bound that some block reaches.
All inputs are finite; a program needn't handle non-finite values.
Results may differ from the reference program's by a relative error of at most 0.017.
Values may be sent and summed in bfloat16 or wider, within the bound.
No kernel may reach another device: no remote copies, remote signals or barrier semaphores. Data moves between devices by JAX's collectives and lax.ppermute only.
A program may use at most 128 MiB of HBM per device.

```python
import math
import jax
import jax.numpy as jnp
import numpy as np
from jax import lax

MODEL_WIDTH = 4096
EXPERT_HIDDEN = 1536
ADAPTER_RANK = 64
TOPK = 4
ROWS = 1024
GROUP_EXPERTS = 16
CAP = 16
ROWS_ALL = 4096
N_GROUP = 4
N_TENSOR = 32


def steps_of(stream_key, dims, pieces, low, largest):
    loudness, own = 1.0, jax.random.fold_in(stream_key, 6)
    for axis_at, shards_of in pieces:
        steps = jnp.exp(jax.random.uniform(jax.random.fold_in(own, axis_at), (shards_of,), jnp.float32, low / len(pieces), largest / len(pieces)))
        loudness = loudness * jnp.repeat(steps, dims[axis_at] // shards_of).reshape([-1 if axis == axis_at else 1 for axis in range(len(dims))])
    return loudness


def assign_block(rng, own, number, rows, amount, top, most, skew):
    sequence = jax.random.permutation(rng, amount)
    heavy_load, usual = load_shares(amount, rows * top, most, skew, True), load_shares(amount, rows * top, most, skew, False)
    places = jnp.arange(amount)

    def named(lengths, rotation):
        used = int((lengths > 0).sum())
        fixed = max(1, used // 4)
        shifted = fixed + (places - fixed + rotation * (used - fixed)) % max(1, amount - fixed)
        return jnp.zeros((amount,), jnp.int32).at[sequence[jnp.where(places < fixed, places, shifted)]].set(jnp.asarray(lengths, jnp.int32))

    lengths = jnp.where(number % 4 == 0, named(heavy_load, number // 4), named(usual, number - number // 4 - 1))
    mixed = jax.random.permutation(jax.random.fold_in(own, 3), amount)
    donor, sink = mixed[0:amount // 2 * 2:2], mixed[1:amount // 2 * 2:2]
    room = jnp.minimum(lengths[donor] - 1, most - lengths[sink]) // 2
    room = jnp.where((donor == sequence[0]) | (sink == sequence[0]) | (lengths[sink] == 0), 0, jnp.maximum(room, 0))
    shifted = jax.random.randint(jax.random.fold_in(own, 4), (amount // 2,), 0, 1 << 20) % (room + 1)
    lengths = lengths.at[donor].add(-shifted).at[sink].add(shifted)
    members = jnp.searchsorted(jnp.cumsum(lengths), jnp.arange(rows * top), side="right").astype(jnp.int32)
    grid = members.reshape(top, rows).T
    grid = grid[jax.random.permutation(jax.random.fold_in(own, 1), rows)]
    rotation = jax.random.randint(jax.random.fold_in(own, 2), (rows, 1), 0, top)
    return jnp.take_along_axis(grid, (jnp.arange(top)[None, :] + rotation) % top, axis=1)


def load_shares(count, total, most, lean, full):
    portions = [(1 << 20) // math.isqrt(grade ** lean) + 1 for grade in range(1, count + 1)]
    largest = most if full else min(most, max(-(-total // count), total * portions[0] // sum(portions)))
    least = 1 if total - largest >= count - 1 else 0
    given, surplus = [largest] + [least] * (count - 1), total - largest - least * (count - 1)
    while surplus > 0:
        free = [i for i in range(1, count) if given[i] < largest] or [i for i in range(1, count) if given[i] < most]
        mass, budget = sum([portions[i] for i in free]), surplus
        for i in free:
            more = min(most - given[i], max(1, budget * portions[i] // mass), surplus)
            given[i] = given[i] + more
            surplus = surplus - more
    return np.array(given)


def centred(stream_key, extent, scale, most, split=(), kind=jnp.bfloat16):
    array = jax.random.normal(stream_key, extent, jnp.float32) * scale
    if len(split) > 0:
        array = steps_of(stream_key, extent, split, -0.22, 0.18) * array
    return jnp.clip(array, min=-most, max=most).astype(kind)


def setup_inputs(seed: int = 0) -> dict:
    streams_of = jax.random.split(jax.random.key(seed), 12)
    tokens = centred(streams_of[0], (ROWS_ALL, MODEL_WIDTH), 1.0, 6.0, ((0, 128),))
    expert_norm_gain = jnp.clip(1.0 + 0.18 * jax.random.normal(streams_of[1], (MODEL_WIDTH,), jnp.float32), 0.1, 1.9)
    routing_keys = jax.random.split(jax.random.fold_in(streams_of[2], 1), ROWS_ALL // (ROWS // N_TENSOR))
    routing_turns = jax.random.permutation(jax.random.fold_in(streams_of[2], 3), ROWS_ALL // (ROWS // N_TENSOR))
    routing = jax.vmap(lambda own, number: assign_block(jax.random.fold_in(streams_of[2], 2), own, number, ROWS // N_TENSOR, GROUP_EXPERTS, TOPK, CAP, 2))(routing_keys, routing_turns).reshape((ROWS_ALL, TOPK))
    chosen_expert_weights = jnp.clip(jnp.exp(math.log(1.0) - 2.9957323 * jax.random.uniform(streams_of[3], (ROWS_ALL, TOPK), jnp.float32) ** steps_of(streams_of[3], (ROWS_ALL, TOPK), ((0, 4),), -0.2, 0.2)), 0.05, 1.0)
    resident_gate_weight = centred(streams_of[4], (MODEL_WIDTH, GROUP_EXPERTS * EXPERT_HIDDEN), MODEL_WIDTH ** -0.5, 0.09375, ((1, 32),))
    resident_up_weight = centred(streams_of[5], (MODEL_WIDTH, GROUP_EXPERTS * EXPERT_HIDDEN), MODEL_WIDTH ** -0.5, 0.09375, ((1, 32),))
    resident_down_weight = centred(streams_of[6], (GROUP_EXPERTS * EXPERT_HIDDEN, MODEL_WIDTH), EXPERT_HIDDEN ** -0.5, 0.15625, ((0, 32),))
    adapter_input_left = centred(streams_of[7], (2, MODEL_WIDTH, GROUP_EXPERTS * ADAPTER_RANK), MODEL_WIDTH ** -0.5, 0.09375, ((1, 4), (2, 32)))
    adapter_input_right = centred(streams_of[8], (2, ADAPTER_RANK, GROUP_EXPERTS * EXPERT_HIDDEN), ADAPTER_RANK ** -0.5, 0.75, ((1, 4), (2, 32)))
    adapter_output_left = centred(streams_of[9], (GROUP_EXPERTS * EXPERT_HIDDEN, ADAPTER_RANK), EXPERT_HIDDEN ** -0.5, 0.15625, ((0, 32), (1, 4)))
    adapter_output_right = centred(streams_of[10], (ADAPTER_RANK, GROUP_EXPERTS * MODEL_WIDTH), ADAPTER_RANK ** -0.5, 0.75, ((0, 4), (1, 32)))
    return {"tokens": tokens, "expert_norm_gain": expert_norm_gain, "routing": routing, "chosen_expert_weights": chosen_expert_weights, "resident_gate_weight": resident_gate_weight, "resident_up_weight": resident_up_weight, "resident_down_weight": resident_down_weight, "adapter_input_left": adapter_input_left, "adapter_input_right": adapter_input_right, "adapter_output_left": adapter_output_left, "adapter_output_right": adapter_output_right}


adapter_scale = 0.5
norm_eps = 1e-06

def normalize(rows_in, expert_norm_gain):
    widened = rows_in.astype(jnp.float32)
    spread = lax.optimization_barrier(jnp.mean(widened * widened, axis=-1, keepdims=True))
    return (widened * lax.rsqrt(spread + norm_eps) * expert_norm_gain).astype(jnp.bfloat16)

def merge_factor_pair(base_matrix, left, right):
    delta_matrix = jnp.dot(left, right, preferred_element_type=jnp.float32)
    return (base_matrix.astype(jnp.float32) + adapter_scale * delta_matrix).astype(jnp.bfloat16)

def slot_table(route_rows, weight_rows, expert_number, capacity):
    chosen = route_rows == expert_number
    routed = jnp.any(chosen, axis=1)
    weight = lax.optimization_barrier(jnp.sum(jnp.where(chosen, weight_rows, jnp.zeros_like(weight_rows)), axis=1))
    slot_place = jnp.cumsum(routed.astype(jnp.int32)) - 1
    target = jnp.where(routed, slot_place, capacity).astype(jnp.int32)
    row_ids = jnp.arange(route_rows.shape[0], dtype=jnp.int32)
    row_index = jnp.zeros((capacity,), jnp.int32).at[target].set(row_ids, mode='drop')
    slot_weight = jnp.zeros((capacity,), weight_rows.dtype).at[target].set(weight, mode='drop')
    return (row_index, slot_weight)

def expert_term(normed, row_index, slot_weight, merged_gate, merged_up, combined_down_weight):
    picked = normed[row_index]
    gate_value = jnp.dot(picked, merged_gate, preferred_element_type=jnp.float32)
    upward = jnp.dot(picked, merged_up, preferred_element_type=jnp.float32)
    hidden = (jax.nn.silu(gate_value) * upward).astype(jnp.bfloat16)
    output = jnp.dot(hidden, combined_down_weight, preferred_element_type=jnp.float32) * slot_weight[:, None]
    output = lax.optimization_barrier(output.astype(jnp.bfloat16)).astype(jnp.float32)
    empty = jnp.zeros((normed.shape[0], normed.shape[1]), jnp.float32)
    return empty.at[row_index].add(output)

def reference(tokens, expert_norm_gain, routing, chosen_expert_weights, resident_gate_weight, resident_up_weight, resident_down_weight, adapter_input_left, adapter_input_right, adapter_output_left, adapter_output_right):
    width_halved = EXPERT_HIDDEN // 2
    group_capacity = min(ROWS, N_TENSOR * CAP)
    normed = normalize(tokens, expert_norm_gain).reshape(N_GROUP, ROWS, MODEL_WIDTH)
    group_routes = routing.reshape(N_GROUP, ROWS, TOPK)
    group_weights = chosen_expert_weights.reshape(N_GROUP, ROWS, TOPK)

    def one_device(totals, device_slot):
        expert_number = device_slot // 2
        column_start = device_slot * width_halved
        input_left_factor = lax.dynamic_slice_in_dim(adapter_input_left, expert_number * ADAPTER_RANK, ADAPTER_RANK, 2)
        input_right_factor = lax.dynamic_slice_in_dim(adapter_input_right, column_start, width_halved, 2)
        merged_gate = merge_factor_pair(lax.dynamic_slice_in_dim(resident_gate_weight, column_start, width_halved, 1), input_left_factor[0], input_right_factor[0])
        merged_up = merge_factor_pair(lax.dynamic_slice_in_dim(resident_up_weight, column_start, width_halved, 1), input_left_factor[1], input_right_factor[1])
        combined_down_weight = merge_factor_pair(lax.dynamic_slice_in_dim(resident_down_weight, column_start, width_halved, 0), lax.dynamic_slice_in_dim(adapter_output_left, column_start, width_halved, 0), lax.dynamic_slice_in_dim(adapter_output_right, expert_number * MODEL_WIDTH, MODEL_WIDTH, 1))
        group_terms = []
        for group_number in range(N_GROUP):
            row_index, slot_weight = slot_table(group_routes[group_number], group_weights[group_number], expert_number, group_capacity)
            group_terms.append(expert_term(normed[group_number], row_index, slot_weight, merged_gate, merged_up, combined_down_weight))
        return (totals + jnp.stack(group_terms), None)
    totals, unused = lax.scan(one_device, jnp.zeros((N_GROUP, ROWS, MODEL_WIDTH), jnp.float32), jnp.arange(N_TENSOR, dtype=jnp.int32))
    return totals.reshape(N_GROUP * ROWS, MODEL_WIDTH).astype(jnp.bfloat16)
```

```python
import functools

import jax
import jax.numpy as jnp
from jax import lax
from jax.experimental import pallas as pl
from jax.experimental.pallas import tpu as pltpu
from jax.sharding import PartitionSpec as P

ADAPTER_SCALE = 0.5
NORM_EPS = 1e-06
EXPERTS = 16
CAP = 16
F32 = jnp.float32
BF16 = jnp.bfloat16
NT = (((1,), (1,)), ((), ()))
TN = (((0,), (0,)), ((), ()))


def exchange(value, axis, bit):
    return lax.ppermute(value, axis, [(i, i ^ bit) for i in range(lax.axis_size(axis))])


def slots_of(route_t, copies):
    rows = route_t.shape[1]
    experts = lax.broadcasted_iota(jnp.int32, (EXPERTS, rows), 0)
    chosen = jnp.zeros((EXPERTS, rows), jnp.bool_)
    for k in range(route_t.shape[0]):
        chosen = chosen | (route_t[k : k + 1, :] == experts)
    upper = (
        lax.broadcasted_iota(jnp.int32, (rows, rows), 0)
        <= lax.broadcasted_iota(jnp.int32, (rows, rows), 1)
    ).astype(F32)
    place = jnp.dot(chosen.astype(F32), upper, preferred_element_type=F32).astype(jnp.int32) - 1
    place = jnp.where(chosen, place, -1)
    slot = lax.broadcasted_iota(jnp.int32, (EXPERTS, copies * CAP, rows), 1) % CAP
    return place[:, None, :] == slot


def dispatch_body(tokens_ref, gain_ref, route_ref, out_ref, normed_ref, mask_ref):
    step = pl.program_id(0)

    @pl.when(step == 0)
    def _():
        wide = tokens_ref[...].astype(F32)
        spread = jnp.mean(wide * wide, axis=-1, keepdims=True)
        normed_ref[...] = (wide * lax.rsqrt(spread + NORM_EPS) * gain_ref[...]).astype(BF16)
        mask = slots_of(route_ref[...], 1)
        mask_ref[...] = mask.astype(F32).reshape(EXPERTS * CAP, -1).astype(BF16)

    per = out_ref.shape[0]
    pick = mask_ref[pl.ds(pl.multiple_of(step * per * CAP, per * CAP), per * CAP), :]
    rows = jnp.dot(pick, normed_ref[...], preferred_element_type=F32).astype(BF16)
    for i in range(per):
        out_ref[i, 0] = rows[i * CAP : (i + 1) * CAP]
        out_ref[i, 1] = rows[i * CAP : (i + 1) * CAP]


def dispatch(tokens, gain, route_t):
    rows, width = tokens.shape
    steps = 4
    per = EXPERTS // steps
    return pl.pallas_call(
        dispatch_body,
        grid=(steps,),
        out_shape=jax.ShapeDtypeStruct((EXPERTS, 2, CAP, width), BF16),
        in_specs=[
            pl.BlockSpec((rows, width), lambda i: (0, 0)),
            pl.BlockSpec((1, width), lambda i: (0, 0)),
            pl.BlockSpec(route_t.shape, lambda i: (0, 0)),
        ],
        out_specs=pl.BlockSpec((per, 2, CAP, width), lambda i: (i, 0, 0, 0)),
        scratch_shapes=[pltpu.VMEM((rows, width), BF16), pltpu.VMEM((EXPERTS * CAP, rows), BF16)],
        compiler_params=pltpu.CompilerParams(vmem_limit_bytes=24 << 20),
        cost_estimate=pl.CostEstimate(
            flops=2 * EXPERTS * CAP * rows * width, bytes_accessed=5 << 20, transcendentals=0
        ),
        name="dispatch",
    )(tokens, gain, route_t)


def ffn_body(
    hid_steps, place_ref, x_ref, wg_ref, wu_ref, wd_ref, own_ref, far_ref, out_ref,
    low_ref, right_ref, hidden_ref, mid_ref, outr_ref,
):
    step = pl.program_id(0)
    group, half = place_ref[0], place_ref[1]
    width = hidden_ref.shape[1]
    block = wg_ref.shape[1]
    packs = (own_ref, far_ref)

    @pl.when(step == 0)
    def _():
        right_ref[...] = jnp.zeros_like(right_ref)
        low = None
        for core in range(2):
            for xh in range(2):
                pack = packs[core]
                there = group ^ (xh * 2 + core)
                near, across = xh * 64, 128 + xh * 48
                span = x_ref.shape[1] // 4
                x = x_ref[:, pl.ds(pl.multiple_of(there * span, span), span)]
                left = jnp.concatenate(
                    [
                        pack[near : near + 32, 0:span],
                        pack[near : near + 32, span : 2 * span],
                        pack[across : across + 32, 0:span],
                        pack[across : across + 32, span : 2 * span],
                    ],
                    axis=0,
                )
                term = lax.dot_general(x, left, NT, preferred_element_type=F32)
                low = term if low is None else low + term
                ranks = (half ^ (there >> 1)) * 64 + (there & 1) * 16
                r0 = pl.multiple_of(ranks, 16)
                r1 = pl.multiple_of(ranks + 32, 16)
                right_ref[pl.ds(r0, 16), 0:width] = pack[near + 48 : near + 64, 0:width]
                right_ref[pl.ds(r1, 16), width : 2 * width] = pack[
                    near + 48 : near + 64, width : 2 * width
                ]
                row = (core * 2 + xh) * 16
                cols = outr_ref.shape[2]
                outr_ref[0, row : row + 16, :] = pack[near + 32 : near + 48, 0:cols]
                outr_ref[1, row : row + 16, :] = pack[across + 32 : across + 48, 0:cols]
        low_ref[...] = (ADAPTER_SCALE * low).astype(BF16)

    for n in range(hid_steps):

        @pl.when(step == n)
        def _(n=n):
            x = x_ref[...]
            low = low_ref[...]
            gate = jnp.dot(x, wg_ref[...], preferred_element_type=F32)
            gate += jnp.dot(
                low, right_ref[:, n * block : (n + 1) * block], preferred_element_type=F32
            )
            up = jnp.dot(x, wu_ref[...], preferred_element_type=F32)
            up += jnp.dot(
                low,
                right_ref[:, width + n * block : width + (n + 1) * block],
                preferred_element_type=F32,
            )
            hidden_ref[:, n * block : (n + 1) * block] = (jax.nn.silu(gate) * up).astype(BF16)

    @pl.when(step == hid_steps)
    def _():
        left = jnp.concatenate(
            [
                packs[core][xh * 64 + 48 : xh * 64 + 64, 2 * width : 3 * width]
                for core in range(2)
                for xh in range(2)
            ],
            axis=0,
        )
        mid = lax.dot_general(hidden_ref[...], left, NT, preferred_element_type=F32)
        mid_ref[...] = (ADAPTER_SCALE * mid).astype(BF16)

    @pl.when(step >= hid_steps)
    def _():
        cols = out_ref.shape[1]
        start = (step - hid_steps) * cols
        side = start // outr_ref.shape[2]
        offset = pl.multiple_of(start - side * outr_ref.shape[2], cols)
        out = jnp.dot(hidden_ref[...], wd_ref[...], preferred_element_type=F32)
        out += jnp.dot(
            mid_ref[...], outr_ref[half ^ side, :, pl.ds(offset, cols)], preferred_element_type=F32
        )
        out_ref[...] = out.astype(BF16)


def feed_forward(place, x, wg, wu, wd, own, far):
    rows, width = x.shape
    hidden = wg.shape[1]
    block, cols = 256, 1024
    hid_steps, out_steps = hidden // block, width // cols
    first = lambda i: jnp.minimum(i, hid_steps - 1)
    later = lambda i: jnp.maximum(i - hid_steps, 0)
    whole = lambda a: pl.BlockSpec(a.shape, lambda i, s: (0,) * a.ndim)
    return pl.pallas_call(
        functools.partial(ffn_body, hid_steps),
        grid_spec=pltpu.PrefetchScalarGridSpec(
            num_scalar_prefetch=1,
            grid=(hid_steps + out_steps,),
            in_specs=[
                whole(x),
                pl.BlockSpec((width, block), lambda i, s: (0, first(i))),
                pl.BlockSpec((width, block), lambda i, s: (0, first(i))),
                pl.BlockSpec((hidden, cols), lambda i, s: (0, later(i))),
                whole(own),
                whole(far),
            ],
            out_specs=pl.BlockSpec((rows, cols), lambda i, s: (0, later(i))),
            scratch_shapes=[
                pltpu.VMEM((rows, 128), BF16),
                pltpu.VMEM((128, 2 * hidden), BF16),
                pltpu.VMEM((rows, hidden), BF16),
                pltpu.VMEM((rows, 64), BF16),
                pltpu.VMEM((2, 64, width // 2), BF16),
            ],
        ),
        out_shape=jax.ShapeDtypeStruct((rows, width), BF16),
        compiler_params=pltpu.CompilerParams(vmem_limit_bytes=48 << 20),
        cost_estimate=pl.CostEstimate(
            flops=6 * rows * width * hidden, bytes_accessed=28 << 20, transcendentals=rows * hidden
        ),
        name="feed_forward",
    )(place, x, wg, wu, wd, own, far)


def combine_body(route_ref, weight_ref, part_ref, out_ref, high_ref, low_ref):
    @pl.when(pl.program_id(0) == 0)
    def _():
        route_t, weight_t = route_ref[...], weight_ref[...]
        rows = route_t.shape[1]
        experts = lax.broadcasted_iota(jnp.int32, (EXPERTS, rows), 0)
        weight = jnp.zeros((EXPERTS, rows), F32)
        for k in range(route_t.shape[0]):
            weight += jnp.where(route_t[k : k + 1, :] == experts, weight_t[k : k + 1, :], 0.0)
        mask = slots_of(route_t, 2)
        spread = jnp.where(mask, weight[:, None, :], 0.0).reshape(2 * EXPERTS * CAP, rows)
        high = spread.astype(BF16)
        high_ref[...] = high
        low_ref[...] = (spread - high.astype(F32)).astype(BF16)

    part = part_ref[...]
    total = lax.dot_general(high_ref[...], part, TN, preferred_element_type=F32)
    total += lax.dot_general(low_ref[...], part, TN, preferred_element_type=F32)
    out_ref[...] = total.astype(BF16)


def combine(route_t, weight_t, part):
    slots, width = part.shape
    rows = route_t.shape[1]
    cols = 1024
    return pl.pallas_call(
        combine_body,
        grid=(width // cols,),
        out_shape=jax.ShapeDtypeStruct((rows, width), BF16),
        in_specs=[
            pl.BlockSpec(route_t.shape, lambda i: (0, 0)),
            pl.BlockSpec(weight_t.shape, lambda i: (0, 0)),
            pl.BlockSpec((slots, cols), lambda i: (0, i)),
        ],
        out_specs=pl.BlockSpec((rows, cols), lambda i: (0, i)),
        scratch_shapes=[pltpu.VMEM((slots, rows), BF16), pltpu.VMEM((slots, rows), BF16)],
        compiler_params=pltpu.CompilerParams(vmem_limit_bytes=24 << 20),
        cost_estimate=pl.CostEstimate(
            flops=4 * slots * rows * width, bytes_accessed=5 << 20, transcendentals=0
        ),
        name="combine",
    )(route_t, weight_t, part)


def gather_factors(input_left, input_right, output_left, output_right):
    left = jnp.transpose(input_left, (2, 0, 1)).reshape(input_left.shape[2], -1)
    right = jnp.concatenate([input_right[0], input_right[1], output_left.T], axis=1)
    wide = right.shape[1]
    pad = lambda a: jnp.pad(a, ((0, 0), (0, wide - a.shape[1])))
    mine = jnp.concatenate([pad(left), pad(output_right), right], axis=0)
    shared = left.shape[0] + output_right.shape[0]
    across_x = exchange(mine, "group", 2)
    partner = exchange(jnp.concatenate([mine[:shared], across_x[:shared]], axis=0), "tensor", 1)
    own = jnp.concatenate([mine, across_x, partner], axis=0)
    return own, exchange(own, "group", 1)


def on_device(
    tokens,
    expert_norm_gain,
    routing,
    chosen_expert_weights,
    resident_gate_weight,
    resident_up_weight,
    resident_down_weight,
    adapter_input_left,
    adapter_input_right,
    adapter_output_left,
    adapter_output_right,
):
    rows, width = tokens.shape
    position = lax.axis_index("tensor")
    place = jnp.stack([lax.axis_index("group"), position % 2]).astype(jnp.int32)
    own, far = gather_factors(
        adapter_input_left, adapter_input_right, adapter_output_left, adapter_output_right
    )
    route_t = lax.dynamic_slice_in_dim(routing, position * rows, rows, 0).T
    weight_t = lax.dynamic_slice_in_dim(chosen_expert_weights, position * rows, rows, 0).T
    sent = dispatch(tokens, expert_norm_gain.reshape(1, width), route_t)
    sent = sent.reshape(2 * EXPERTS, CAP, width)
    x = lax.all_to_all(sent, "tensor", 0, 0, tiled=True).reshape(2 * EXPERTS * CAP, width)
    part = feed_forward(
        place, x, resident_gate_weight, resident_up_weight, resident_down_weight, own, far
    )
    part = part.reshape(2 * EXPERTS, CAP, width)
    back = lax.all_to_all(part, "tensor", 0, 0, tiled=True).reshape(2 * EXPERTS * CAP, width)
    return combine(route_t, weight_t, back)


def solution(mesh):
    return jax.shard_map(
        on_device,
        mesh=mesh,
        in_specs=(
            P(("group", "tensor"), None),
            P(),
            P("group", None),
            P("group", None),
            P(None, "tensor"),
            P(None, "tensor"),
            P("tensor", None),
            P(None, "group", "tensor"),
            P(None, "group", "tensor"),
            P("tensor", "group"),
            P("group", "tensor"),
        ),
        out_specs=P(("group", "tensor"), None),
        check_vma=False,
    )
```

```python
import functools

import jax
import jax.numpy as jnp
from jax import lax
from jax.experimental import pallas as pl
from jax.experimental.pallas import tpu as pltpu
from jax.sharding import PartitionSpec as P

ADAPTER_SCALE = 0.5
NORM_EPS = 1e-06
EXPERTS = 16
CAP = 16
PART = CAP // 2
FFN_VMEM = 50 << 20
DISPATCH_VMEM = 60 << 20
F32 = jnp.float32
BF16 = jnp.bfloat16
NT = (((1,), (1,)), ((), ()))
TN = (((0,), (0,)), ((), ()))


def exchange(value, axis, bit):
    return lax.ppermute(value, axis, [(i, i ^ bit) for i in range(lax.axis_size(axis))])


def slots_of(route_t, depth, copies, first):
    rows = route_t.shape[1]
    experts = lax.broadcasted_iota(jnp.int32, (EXPERTS, rows), 0)
    chosen = jnp.zeros((EXPERTS, rows), jnp.bool_)
    for k in range(route_t.shape[0]):
        chosen = chosen | (route_t[k : k + 1, :] == experts)
    upper = (
        lax.broadcasted_iota(jnp.int32, (rows, rows), 0)
        <= lax.broadcasted_iota(jnp.int32, (rows, rows), 1)
    ).astype(F32)
    place = jnp.dot(chosen.astype(F32), upper, preferred_element_type=F32).astype(jnp.int32) - 1
    place = jnp.where(chosen, place, -1)
    slot = lax.broadcasted_iota(jnp.int32, (EXPERTS, copies * depth, rows), 1) % depth
    return place[:, None, :] == slot + first


def dispatch_body(tokens_ref, gain_ref, route_ref, early_ref, late_ref, normed_ref, mask_ref):
    step = pl.program_id(0)

    @pl.when(step == 0)
    def _():
        wide = tokens_ref[...].astype(F32)
        spread = jnp.mean(wide * wide, axis=-1, keepdims=True)
        normed_ref[...] = (wide * lax.rsqrt(spread + NORM_EPS) * gain_ref[...]).astype(BF16)
        mask = slots_of(route_ref[...], CAP, 1, 0)
        mask_ref[...] = mask.astype(F32).reshape(EXPERTS * CAP, -1).astype(BF16)

    per = early_ref.shape[0]
    pick = mask_ref[pl.ds(pl.multiple_of(step * per * CAP, per * CAP), per * CAP), :]
    rows = jnp.dot(pick, normed_ref[...], preferred_element_type=F32)
    for i in range(per):
        for half in range(2):
            early_ref[i, half] = rows[i * CAP : i * CAP + PART].astype(BF16)
            late_ref[i, half] = rows[i * CAP + PART : (i + 1) * CAP].astype(BF16)


def dispatch(tokens, gain, route_t):
    rows, width = tokens.shape
    steps = 4
    per = EXPERTS // steps
    sent = pltpu.HBM((EXPERTS, 2, PART, width), BF16)
    out_spec = pl.BlockSpec((per, 2, PART, width), lambda i: (i, 0, 0, 0))
    return pl.pallas_call(
        dispatch_body,
        grid=(steps,),
        out_shape=(sent, sent),
        in_specs=[
            pl.BlockSpec((rows, width), lambda i: (0, 0)),
            pl.BlockSpec((1, width), lambda i: (0, 0)),
            pl.BlockSpec(route_t.shape, lambda i: (0, 0)),
        ],
        out_specs=(out_spec, out_spec),
        scratch_shapes=[pltpu.VMEM((rows, width), BF16), pltpu.VMEM((EXPERTS * CAP, rows), BF16)],
        compiler_params=pltpu.CompilerParams(vmem_limit_bytes=DISPATCH_VMEM),
        cost_estimate=pl.CostEstimate(
            flops=2 * EXPERTS * CAP * rows * width, bytes_accessed=5 << 20, transcendentals=0
        ),
        name="dispatch",
    )(tokens, gain, route_t)


def ffn_body(
    hid_steps, place_ref, x_ref, wg_ref, wu_ref, wd_ref, own_ref, far_ref, out_ref,
    low_ref, right_ref, hidden_ref, mid_ref, outr_ref,
):
    step = pl.program_id(0)
    group, half = place_ref[0], place_ref[1]
    width = hidden_ref.shape[1]
    block = wg_ref.shape[1]
    packs = (own_ref, far_ref)

    @pl.when(step == 0)
    def _():
        right_ref[...] = jnp.zeros_like(right_ref)
        low = None
        for core in range(2):
            for xh in range(2):
                pack = packs[core]
                there = group ^ (xh * 2 + core)
                near, across = xh * 64, 128 + xh * 48
                span = x_ref.shape[1] // 4
                x = x_ref[:, pl.ds(pl.multiple_of(there * span, span), span)]
                left = jnp.concatenate(
                    [
                        pack[near : near + 32, 0:span],
                        pack[near : near + 32, span : 2 * span],
                        pack[across : across + 32, 0:span],
                        pack[across : across + 32, span : 2 * span],
                    ],
                    axis=0,
                )
                term = lax.dot_general(x, left, NT, preferred_element_type=F32)
                low = term if low is None else low + term
                ranks = (half ^ (there >> 1)) * 64 + (there & 1) * 16
                r0 = pl.multiple_of(ranks, 16)
                r1 = pl.multiple_of(ranks + 32, 16)
                right_ref[pl.ds(r0, 16), 0:width] = pack[near + 48 : near + 64, 0:width]
                right_ref[pl.ds(r1, 16), width : 2 * width] = pack[
                    near + 48 : near + 64, width : 2 * width
                ]
                row = (core * 2 + xh) * 16
                cols = outr_ref.shape[2]
                outr_ref[0, row : row + 16, :] = pack[near + 32 : near + 48, 0:cols]
                outr_ref[1, row : row + 16, :] = pack[across + 32 : across + 48, 0:cols]
        low_ref[...] = (ADAPTER_SCALE * low).astype(BF16)

    for n in range(hid_steps):

        @pl.when(step == n)
        def _(n=n):
            x = x_ref[...]
            low = low_ref[...]
            gate = jnp.dot(x, wg_ref[...], preferred_element_type=F32)
            gate += jnp.dot(
                low, right_ref[:, n * block : (n + 1) * block], preferred_element_type=F32
            )
            up = jnp.dot(x, wu_ref[...], preferred_element_type=F32)
            up += jnp.dot(
                low,
                right_ref[:, width + n * block : width + (n + 1) * block],
                preferred_element_type=F32,
            )
            hidden_ref[:, n * block : (n + 1) * block] = (jax.nn.silu(gate) * up).astype(BF16)

    @pl.when(step == hid_steps)
    def _():
        left = jnp.concatenate(
            [
                packs[core][xh * 64 + 48 : xh * 64 + 64, 2 * width : 3 * width]
                for core in range(2)
                for xh in range(2)
            ],
            axis=0,
        )
        mid = lax.dot_general(hidden_ref[...], left, NT, preferred_element_type=F32)
        mid_ref[...] = (ADAPTER_SCALE * mid).astype(BF16)

    @pl.when(step >= hid_steps)
    def _():
        cols = out_ref.shape[1]
        start = (step - hid_steps) * cols
        side = start // outr_ref.shape[2]
        offset = pl.multiple_of(start - side * outr_ref.shape[2], cols)
        out = jnp.dot(hidden_ref[...], wd_ref[...], preferred_element_type=F32)
        out += jnp.dot(
            mid_ref[...], outr_ref[half ^ side, :, pl.ds(offset, cols)], preferred_element_type=F32
        )
        out_ref[...] = out.astype(BF16)


def feed_forward(place, x, wg, wu, wd, own, far):
    rows, width = x.shape
    hidden = wg.shape[1]
    block, cols = 256, 1024
    hid_steps, out_steps = hidden // block, width // cols
    first = lambda i: jnp.minimum(i, hid_steps - 1)
    later = lambda i: jnp.maximum(i - hid_steps, 0)
    whole = lambda a: pl.BlockSpec(a.shape, lambda i, s: (0,) * a.ndim)
    return pl.pallas_call(
        functools.partial(ffn_body, hid_steps),
        grid_spec=pltpu.PrefetchScalarGridSpec(
            num_scalar_prefetch=1,
            grid=(hid_steps + out_steps,),
            in_specs=[
                whole(x),
                pl.BlockSpec((width, block), lambda i, s: (0, first(i))),
                pl.BlockSpec((width, block), lambda i, s: (0, first(i))),
                pl.BlockSpec((hidden, cols), lambda i, s: (0, later(i))),
                whole(own),
                whole(far),
            ],
            out_specs=pl.BlockSpec((rows, cols), lambda i, s: (0, later(i))),
            scratch_shapes=[
                pltpu.VMEM((rows, 128), BF16),
                pltpu.VMEM((128, 2 * hidden), BF16),
                pltpu.VMEM((rows, hidden), BF16),
                pltpu.VMEM((rows, 64), BF16),
                pltpu.VMEM((2, 64, width // 2), BF16),
            ],
        ),
        out_shape=pltpu.HBM((rows, width), BF16),
        compiler_params=pltpu.CompilerParams(vmem_limit_bytes=FFN_VMEM),
        cost_estimate=pl.CostEstimate(
            flops=6 * rows * width * hidden, bytes_accessed=28 << 20, transcendentals=rows * hidden
        ),
        name="feed_forward",
    )(place, x, wg, wu, wd, own, far)


def combine_body(first, route_ref, weight_ref, part_ref, *refs):
    base_ref = refs[0] if len(refs) == 4 else None
    out_ref, high_ref, low_ref = refs[-3:]

    @pl.when(pl.program_id(0) == 0)
    def _():
        route_t, weight_t = route_ref[...], weight_ref[...]
        rows = route_t.shape[1]
        experts = lax.broadcasted_iota(jnp.int32, (EXPERTS, rows), 0)
        weight = jnp.zeros((EXPERTS, rows), F32)
        for k in range(route_t.shape[0]):
            weight += jnp.where(route_t[k : k + 1, :] == experts, weight_t[k : k + 1, :], 0.0)
        mask = slots_of(route_t, PART, 2, first)
        spread = jnp.where(mask, weight[:, None, :], 0.0).reshape(2 * EXPERTS * PART, rows)
        high = spread.astype(BF16)
        high_ref[...] = high
        low_ref[...] = (spread - high.astype(F32)).astype(BF16)

    part = part_ref[...]
    total = lax.dot_general(high_ref[...], part, TN, preferred_element_type=F32)
    total += lax.dot_general(low_ref[...], part, TN, preferred_element_type=F32)
    if base_ref is not None:
        total += base_ref[...]
    out_ref[...] = total.astype(out_ref.dtype)


def combine(route_t, weight_t, part, first, base, out_type):
    slots, width = part.shape
    rows = route_t.shape[1]
    cols = 1024
    sheet = pl.BlockSpec((rows, cols), lambda i: (0, i))
    in_specs = [
        pl.BlockSpec(route_t.shape, lambda i: (0, 0)),
        pl.BlockSpec(weight_t.shape, lambda i: (0, 0)),
        pl.BlockSpec((slots, cols), lambda i: (0, i)),
    ]
    operands = (route_t, weight_t, part)
    if base is not None:
        in_specs.append(sheet)
        operands += (base,)
    return pl.pallas_call(
        functools.partial(combine_body, first),
        grid=(width // cols,),
        out_shape=jax.ShapeDtypeStruct((rows, width), out_type),
        in_specs=in_specs,
        out_specs=sheet,
        scratch_shapes=[pltpu.VMEM((slots, rows), BF16), pltpu.VMEM((slots, rows), BF16)],
        compiler_params=pltpu.CompilerParams(vmem_limit_bytes=24 << 20),
        cost_estimate=pl.CostEstimate(
            flops=4 * slots * rows * width, bytes_accessed=3 << 20, transcendentals=0
        ),
        name="combine",
    )(*operands)


def gather_factors(input_left, input_right, output_left, output_right):
    left = jnp.transpose(input_left, (2, 0, 1)).reshape(input_left.shape[2], -1)
    right = jnp.concatenate([input_right[0], input_right[1], output_left.T], axis=1)
    wide = right.shape[1]
    pad = lambda a: jnp.pad(a, ((0, 0), (0, wide - a.shape[1])))
    mine = jnp.concatenate([pad(left), pad(output_right), right], axis=0)
    shared = left.shape[0] + output_right.shape[0]
    groups, tensor = lax.axis_size("group"), lax.axis_size("tensor")
    both = [
        (g * tensor + t, (g ^ 2) * tensor + (t ^ 1)) for g in range(groups) for t in range(tensor)
    ]
    across_x = exchange(mine, "group", 2)
    partner = exchange(mine[:shared], "tensor", 1)
    corner = lax.ppermute(mine[:shared], ("group", "tensor"), both)
    return mine, across_x, partner, corner


def on_device(
    tokens,
    expert_norm_gain,
    routing,
    chosen_expert_weights,
    resident_gate_weight,
    resident_up_weight,
    resident_down_weight,
    adapter_input_left,
    adapter_input_right,
    adapter_output_left,
    adapter_output_right,
):
    rows, width = tokens.shape
    position = lax.axis_index("tensor")
    place = jnp.stack([lax.axis_index("group"), position % 2]).astype(jnp.int32)
    pieces = gather_factors(
        adapter_input_left, adapter_input_right, adapter_output_left, adapter_output_right
    )
    route_t = lax.dynamic_slice_in_dim(routing, position * rows, rows, 0).T
    weight_t = lax.dynamic_slice_in_dim(chosen_expert_weights, position * rows, rows, 0).T
    sent = dispatch(tokens, expert_norm_gain.reshape(1, width), route_t)

    def travel(value):
        value = value.reshape(2 * EXPERTS, PART, width)
        return lax.all_to_all(value, "tensor", 0, 0, tiled=True).reshape(-1, width)

    weights = (resident_gate_weight, resident_up_weight, resident_down_weight)
    arrived = [travel(value) for value in sent]
    *pieces, arrived[0] = lax.optimization_barrier((*pieces, arrived[0]))
    own = jnp.concatenate(pieces, axis=0)
    far = exchange(own, "group", 1)
    parts = [travel(feed_forward(place, x, *weights, own, far)) for x in arrived]
    base = combine(route_t, weight_t, parts[0], 0, None, F32)
    return combine(route_t, weight_t, parts[1], PART, base, BF16)


def solution(mesh):
    return jax.shard_map(
        on_device,
        mesh=mesh,
        in_specs=(
            P(("group", "tensor"), None),
            P(),
            P("group", None),
            P("group", None),
            P(None, "tensor"),
            P(None, "tensor"),
            P("tensor", None),
            P(None, "group", "tensor"),
            P(None, "group", "tensor"),
            P("tensor", "group"),
            P("group", "tensor"),
        ),
        out_specs=P(("group", "tensor"), None),
        check_vma=False,
    )
```

```python
import functools

import jax
import jax.numpy as jnp
from jax import lax
from jax.experimental import pallas as pl
from jax.experimental.pallas import tpu as pltpu
from jax.sharding import PartitionSpec as P

ADAPTER_SCALE = 0.5
NORM_EPS = 1e-06
EXPERTS = 16
CAP = 16
PART = CAP // 2
FFN_VMEM = (50 << 20, 62 << 20)
ROWS_AT = ((0, 128), (64, 176))
DISPATCH_VMEM = 64 << 20
F32 = jnp.float32
BF16 = jnp.bfloat16
NT = (((1,), (1,)), ((), ()))
TN = (((0,), (0,)), ((), ()))


def exchange(value, axis, bit):
    return lax.ppermute(value, axis, [(i, i ^ bit) for i in range(lax.axis_size(axis))])


def own_rows(table_ref, rows):
    position = lax.axis_index("tensor")
    per = 128 // rows
    start = pl.multiple_of((position // per) * 128, 128)
    block = table_ref[:, pl.ds(start, 128)]
    return pltpu.roll(block, (128 - (position % per) * rows) % 128, 1)[:, 0:rows]


def slots_of(route_t, depth, copies, first):
    rows = route_t.shape[1]
    experts = lax.broadcasted_iota(jnp.int32, (EXPERTS, rows), 0)
    chosen = jnp.zeros((EXPERTS, rows), jnp.bool_)
    for k in range(route_t.shape[0]):
        chosen = chosen | (route_t[k : k + 1, :] == experts)
    upper = (
        lax.broadcasted_iota(jnp.int32, (rows, rows), 0)
        <= lax.broadcasted_iota(jnp.int32, (rows, rows), 1)
    ).astype(F32)
    place = jnp.dot(chosen.astype(F32), upper, preferred_element_type=F32).astype(jnp.int32) - 1
    place = jnp.where(chosen, place, -1)
    slot = lax.broadcasted_iota(jnp.int32, (EXPERTS, copies * depth, rows), 1) % depth
    return place[:, None, :] == slot + first


def dispatch_body(first, tokens_ref, gain_ref, route_ref, out_ref, normed_ref, mask_ref):
    step = pl.program_id(0)

    @pl.when(step == 0)
    def _():
        wide = tokens_ref[...].astype(F32)
        spread = jnp.mean(wide * wide, axis=-1, keepdims=True)
        normed_ref[...] = (wide * lax.rsqrt(spread + NORM_EPS) * gain_ref[...]).astype(BF16)
        mask = slots_of(own_rows(route_ref, tokens_ref.shape[0]), PART, 1, first)
        mask_ref[...] = mask.astype(F32).reshape(EXPERTS * PART, -1).astype(BF16)

    per = out_ref.shape[0]
    pick = mask_ref[pl.ds(pl.multiple_of(step * per * PART, per * PART), per * PART), :]
    rows = jnp.dot(pick, normed_ref[...], preferred_element_type=F32)
    for i in range(per):
        for half in range(2):
            out_ref[i, half] = rows[i * PART : (i + 1) * PART].astype(BF16)


def dispatch(tokens, gain, route_t, first):
    rows, width = tokens.shape
    steps = 4
    per = EXPERTS // steps
    return pl.pallas_call(
        functools.partial(dispatch_body, first),
        grid=(steps,),
        out_shape=pltpu.HBM((EXPERTS, 2, PART, width), BF16),
        in_specs=[
            pl.BlockSpec((rows, width), lambda i: (0, 0)),
            pl.BlockSpec((1, width), lambda i: (0, 0)),
            pl.BlockSpec(route_t.shape, lambda i: (0, 0)),
        ],
        out_specs=pl.BlockSpec((per, 2, PART, width), lambda i: (i, 0, 0, 0)),
        scratch_shapes=[pltpu.VMEM((rows, width), BF16), pltpu.VMEM((EXPERTS * PART, rows), BF16)],
        compiler_params=pltpu.CompilerParams(vmem_limit_bytes=DISPATCH_VMEM),
        cost_estimate=pl.CostEstimate(
            flops=2 * EXPERTS * PART * rows * width, bytes_accessed=3 << 20, transcendentals=0
        ),
        name="dispatch",
    )(tokens, gain, route_t)


def mixing_body(rows, route_ref, weight_ref, out_ref):
    route_t, weight_t = own_rows(route_ref, rows), own_rows(weight_ref, rows)
    experts = lax.broadcasted_iota(jnp.int32, (EXPERTS, rows), 0)
    weight = jnp.zeros((EXPERTS, rows), F32)
    for k in range(route_t.shape[0]):
        weight += jnp.where(route_t[k : k + 1, :] == experts, weight_t[k : k + 1, :], 0.0)
    for part in range(CAP // PART):
        mask = slots_of(route_t, PART, 2, part * PART)
        spread = jnp.where(mask, weight[:, None, :], 0.0).reshape(2 * EXPERTS * PART, rows).T
        high = spread.astype(BF16)
        out_ref[part, 0:rows, :] = high
        out_ref[part, rows : 2 * rows, :] = (spread - high.astype(F32)).astype(BF16)


def mixing(route_t, weight_t, rows):
    vmem = pl.BlockSpec(memory_space=pltpu.VMEM)
    return pl.pallas_call(
        functools.partial(mixing_body, rows),
        in_specs=[vmem, vmem],
        out_specs=vmem,
        out_shape=jax.ShapeDtypeStruct((CAP // PART, 2 * rows, 2 * EXPERTS * PART), BF16),
        cost_estimate=pl.CostEstimate(flops=1 << 20, bytes_accessed=1 << 17, transcendentals=0),
        name="mixing",
    )(route_t, weight_t)


def ffn_body(
    place_ref, x_ref, wg_ref, wu_ref, wd_ref, own_ref, far_ref, out_ref,
    gate_ref, up_ref, low_ref, right_ref, hidden_ref, mid_ref, outr_ref,
):
    step = pl.program_id(0)
    group, half = place_ref[0], place_ref[1]
    width = hidden_ref.shape[1]
    span = x_ref.shape[1]
    packs = (own_ref, far_ref)

    for turn in range(4):

        @pl.when(step == turn)
        def _(turn=turn):
            xh, pack = turn // 2, packs[turn % 2]
            there = group ^ turn
            near, across = ROWS_AT[xh]
            x = x_ref[...]
            left = jnp.concatenate(
                [
                    pack[near : near + 32, 0:span],
                    pack[near : near + 32, span : 2 * span],
                    pack[across : across + 32, 0:span],
                    pack[across : across + 32, span : 2 * span],
                ],
                axis=0,
            )
            gate = jnp.dot(x, wg_ref[...], preferred_element_type=F32)
            up = jnp.dot(x, wu_ref[...], preferred_element_type=F32)
            low = lax.dot_general(x, left, NT, preferred_element_type=F32)
            if turn == 0:
                right_ref[...] = jnp.zeros_like(right_ref)
            else:
                gate += gate_ref[...]
                up += up_ref[...]
                low += low_ref[...]
            ranks = (half ^ (there >> 1)) * 64 + (there & 1) * 16
            r0 = pl.multiple_of(ranks, 16)
            r1 = pl.multiple_of(ranks + 32, 16)
            right_ref[pl.ds(r0, 16), 0:width] = pack[near + 48 : near + 64, 0:width]
            right_ref[pl.ds(r1, 16), width : 2 * width] = pack[
                near + 48 : near + 64, width : 2 * width
            ]
            cols = outr_ref.shape[2]
            outr_ref[0, turn * 16 : turn * 16 + 16, :] = pack[near + 32 : near + 48, 0:cols]
            outr_ref[1, turn * 16 : turn * 16 + 16, :] = pack[across + 32 : across + 48, 0:cols]
            if turn < 3:
                gate_ref[...], up_ref[...], low_ref[...] = gate, up, low
                return
            scaled = (ADAPTER_SCALE * low).astype(BF16)
            gate += jnp.dot(scaled, right_ref[:, 0:width], preferred_element_type=F32)
            up += jnp.dot(scaled, right_ref[:, width : 2 * width], preferred_element_type=F32)
            hidden = (jax.nn.silu(gate) * up).astype(BF16)
            hidden_ref[...] = hidden
            left = jnp.concatenate(
                [
                    packs[t % 2][
                        ROWS_AT[t // 2][0] + 48 : ROWS_AT[t // 2][0] + 64, 2 * width : 3 * width
                    ]
                    for t in range(4)
                ],
                axis=0,
            )
            mid = lax.dot_general(hidden, left, NT, preferred_element_type=F32)
            mid_ref[...] = (ADAPTER_SCALE * mid).astype(BF16)

    @pl.when(step >= 4)
    def _():
        cols = out_ref.shape[1]
        start = (step - 4) * cols
        side = start // outr_ref.shape[2]
        offset = pl.multiple_of(start - side * outr_ref.shape[2], cols)
        out = jnp.dot(hidden_ref[...], wd_ref[...], preferred_element_type=F32)
        out += jnp.dot(
            mid_ref[...], outr_ref[half ^ side, :, pl.ds(offset, cols)], preferred_element_type=F32
        )
        out_ref[...] = out.astype(BF16)


def feed_forward(place, x, wg, wu, wd, own, far, limit):
    rows, width = x.shape
    hidden = wg.shape[1]
    span, cols = width // 4, 1024
    turn = lambda i, s: s[0] ^ jnp.minimum(i, 3)
    later = lambda i: jnp.maximum(i - 4, 0)
    whole = lambda a: pl.BlockSpec(a.shape, lambda i, s: (0,) * a.ndim)
    return pl.pallas_call(
        ffn_body,
        grid_spec=pltpu.PrefetchScalarGridSpec(
            num_scalar_prefetch=1,
            grid=(4 + width // cols,),
            in_specs=[
                pl.BlockSpec((rows, span), lambda i, s: (0, turn(i, s))),
                pl.BlockSpec((span, hidden), lambda i, s: (turn(i, s), 0)),
                pl.BlockSpec((span, hidden), lambda i, s: (turn(i, s), 0)),
                pl.BlockSpec((hidden, cols), lambda i, s: (0, later(i))),
                whole(own),
                whole(far),
            ],
            out_specs=pl.BlockSpec((rows, cols), lambda i, s: (0, later(i))),
            scratch_shapes=[
                pltpu.VMEM((rows, hidden), F32),
                pltpu.VMEM((rows, hidden), F32),
                pltpu.VMEM((rows, 128), F32),
                pltpu.VMEM((128, 2 * hidden), BF16),
                pltpu.VMEM((rows, hidden), BF16),
                pltpu.VMEM((rows, 64), BF16),
                pltpu.VMEM((2, 64, width // 2), BF16),
            ],
        ),
        out_shape=pltpu.HBM((rows, width), BF16),
        compiler_params=pltpu.CompilerParams(vmem_limit_bytes=limit),
        cost_estimate=pl.CostEstimate(
            flops=6 * rows * width * hidden, bytes_accessed=28 << 20, transcendentals=rows * hidden
        ),
        name="feed_forward",
    )(place, x, wg, wu, wd, own, far)


def combine_body(mix_ref, part_ref, *refs):
    out_ref = refs[-1]
    rows = out_ref.shape[0]
    both = jnp.dot(mix_ref[...], part_ref[...], preferred_element_type=F32)
    total = both[0:rows] + both[rows : 2 * rows]
    if len(refs) == 2:
        total += refs[0][...]
    out_ref[...] = total.astype(out_ref.dtype)


def combine(mix, part, base, out_type):
    slots, width = part.shape
    rows = mix.shape[0] // 2
    cols = 1024
    sheet = pl.BlockSpec((rows, cols), lambda i: (0, i))
    in_specs = [
        pl.BlockSpec(mix.shape, lambda i: (0, 0)),
        pl.BlockSpec((slots, cols), lambda i: (0, i)),
    ]
    operands = (mix, part)
    if base is not None:
        in_specs.append(sheet)
        operands += (base,)
    return pl.pallas_call(
        combine_body,
        grid=(width // cols,),
        out_shape=jax.ShapeDtypeStruct((rows, width), out_type),
        in_specs=in_specs,
        out_specs=sheet,
        compiler_params=pltpu.CompilerParams(vmem_limit_bytes=24 << 20),
        cost_estimate=pl.CostEstimate(
            flops=4 * slots * rows * width, bytes_accessed=3 << 20, transcendentals=0
        ),
        name="combine",
    )(*operands)


def gather_factors(input_left, input_right, output_left, output_right):
    left = jnp.transpose(input_left, (2, 0, 1)).reshape(input_left.shape[2], -1)
    right = jnp.concatenate([input_right[0], input_right[1], output_left.T], axis=1)
    wide = right.shape[1]
    pad = lambda a: jnp.pad(a, ((0, 0), (0, wide - a.shape[1])))
    mine = jnp.concatenate([pad(left), pad(output_right), right], axis=0)
    shared = left.shape[0] + output_right.shape[0]
    groups, tensor = lax.axis_size("group"), lax.axis_size("tensor")
    both = [
        (g * tensor + t, (g ^ 2) * tensor + (t ^ 1)) for g in range(groups) for t in range(tensor)
    ]
    across_x = exchange(mine, "group", 2)
    partner = exchange(mine[:shared], "tensor", 1)
    corner = lax.ppermute(mine[:shared], ("group", "tensor"), both)
    return mine, across_x, partner, corner


def on_device(
    tokens,
    expert_norm_gain,
    routing,
    chosen_expert_weights,
    resident_gate_weight,
    resident_up_weight,
    resident_down_weight,
    adapter_input_left,
    adapter_input_right,
    adapter_output_left,
    adapter_output_right,
):
    rows, width = tokens.shape
    position = lax.axis_index("tensor")
    place = jnp.stack([lax.axis_index("group"), position % 2]).astype(jnp.int32)
    pieces = gather_factors(
        adapter_input_left, adapter_input_right, adapter_output_left, adapter_output_right
    )
    route_t, gain = routing.T, expert_norm_gain.reshape(1, width)
    sent = [dispatch(tokens, gain, route_t, first) for first in range(0, CAP, PART)]
    mix = mixing(route_t, chosen_expert_weights.T, rows)

    def travel(value):
        value = value.reshape(2 * EXPERTS, PART, width)
        return lax.all_to_all(value, "tensor", 0, 0, tiled=True).reshape(-1, width)

    weights = (resident_gate_weight, resident_up_weight, resident_down_weight)
    arrived = [travel(value) for value in sent]
    *pieces, arrived[0] = lax.optimization_barrier((*pieces, arrived[0]))
    own = jnp.concatenate(pieces, axis=0)
    far = exchange(own, "group", 1)
    parts = [
        travel(feed_forward(place, x, *weights, own, far, limit))
        for x, limit in zip(arrived, FFN_VMEM)
    ]
    base = combine(mix[0], parts[0], None, F32)
    return combine(mix[1], parts[1], base, BF16)


def solution(mesh):
    return jax.shard_map(
        on_device,
        mesh=mesh,
        in_specs=(
            P(("group", "tensor"), None),
            P(),
            P("group", None),
            P("group", None),
            P(None, "tensor"),
            P(None, "tensor"),
            P("tensor", None),
            P(None, "group", "tensor"),
            P(None, "group", "tensor"),
            P("tensor", "group"),
            P("group", "tensor"),
        ),
        out_specs=P(("group", "tensor"), None),
        check_vma=False,
    )
```

```python
import functools

import jax
import jax.numpy as jnp
from jax import lax
from jax.experimental import pallas as pl
from jax.experimental.pallas import tpu as pltpu
from jax.sharding import PartitionSpec as P

ADAPTER_SCALE = 0.5
NORM_EPS = 1e-06
EXPERTS = 16
CAP = 16
PART = CAP // 2
FFN_VMEM = (50 << 20, 62 << 20)
ROWS_AT = ((0, 128), (64, 176))
DISPATCH_VMEM = 64 << 20
F32 = jnp.float32
BF16 = jnp.bfloat16
NT = (((1,), (1,)), ((), ()))
TN = (((0,), (0,)), ((), ()))


def exchange(value, axis, bit):
    return lax.ppermute(value, axis, [(i, i ^ bit) for i in range(lax.axis_size(axis))])


def own_rows(table_ref, rows):
    position = lax.axis_index("tensor")
    per = 128 // rows
    start = pl.multiple_of((position // per) * 128, 128)
    block = table_ref[:, pl.ds(start, 128)]
    return pltpu.roll(block, (128 - (position % per) * rows) % 128, 1)[:, 0:rows]


def slots_of(route_t, depth, copies, first):
    rows = route_t.shape[1]
    experts = lax.broadcasted_iota(jnp.int32, (EXPERTS, rows), 0)
    chosen = jnp.zeros((EXPERTS, rows), jnp.bool_)
    for k in range(route_t.shape[0]):
        chosen = chosen | (route_t[k : k + 1, :] == experts)
    upper = (
        lax.broadcasted_iota(jnp.int32, (rows, rows), 0)
        <= lax.broadcasted_iota(jnp.int32, (rows, rows), 1)
    ).astype(F32)
    place = jnp.dot(chosen.astype(F32), upper, preferred_element_type=F32).astype(jnp.int32) - 1
    place = jnp.where(chosen, place, -1)
    slot = lax.broadcasted_iota(jnp.int32, (EXPERTS, copies * depth, rows), 1) % depth
    return place[:, None, :] == slot + first


def dispatch_body(first, tokens_ref, gain_ref, route_ref, out_ref, normed_ref, mask_ref):
    step = pl.program_id(0)

    @pl.when(step == 0)
    def _():
        wide = tokens_ref[...].astype(F32)
        spread = jnp.mean(wide * wide, axis=-1, keepdims=True)
        normed_ref[...] = (wide * lax.rsqrt(spread + NORM_EPS) * gain_ref[...]).astype(BF16)
        mask = slots_of(own_rows(route_ref, tokens_ref.shape[0]), PART, 1, first)
        mask_ref[...] = mask.astype(F32).reshape(EXPERTS * PART, -1).astype(BF16)

    per = out_ref.shape[0]
    pick = mask_ref[pl.ds(pl.multiple_of(step * per * PART, per * PART), per * PART), :]
    rows = jnp.dot(pick, normed_ref[...], preferred_element_type=F32)
    for i in range(per):
        for half in range(2):
            out_ref[i, half] = rows[i * PART : (i + 1) * PART].astype(BF16)


def dispatch(tokens, gain, route_t, first):
    rows, width = tokens.shape
    steps = 2
    per = EXPERTS // steps
    return pl.pallas_call(
        functools.partial(dispatch_body, first),
        grid=(steps,),
        out_shape=pltpu.HBM((EXPERTS, 2, PART, width), BF16),
        in_specs=[
            pl.BlockSpec((rows, width), lambda i: (0, 0)),
            pl.BlockSpec((1, width), lambda i: (0, 0)),
            pl.BlockSpec(route_t.shape, lambda i: (0, 0)),
        ],
        out_specs=pl.BlockSpec((per, 2, PART, width), lambda i: (i, 0, 0, 0)),
        scratch_shapes=[pltpu.VMEM((rows, width), BF16), pltpu.VMEM((EXPERTS * PART, rows), BF16)],
        compiler_params=pltpu.CompilerParams(vmem_limit_bytes=DISPATCH_VMEM),
        cost_estimate=pl.CostEstimate(
            flops=2 * EXPERTS * PART * rows * width, bytes_accessed=3 << 20, transcendentals=0
        ),
        name="dispatch",
    )(tokens, gain, route_t)


def mixing_body(rows, route_ref, weight_ref, out_ref):
    route_t, weight_t = own_rows(route_ref, rows), own_rows(weight_ref, rows)
    experts = lax.broadcasted_iota(jnp.int32, (EXPERTS, rows), 0)
    weight = jnp.zeros((EXPERTS, rows), F32)
    for k in range(route_t.shape[0]):
        weight += jnp.where(route_t[k : k + 1, :] == experts, weight_t[k : k + 1, :], 0.0)
    for part in range(CAP // PART):
        mask = slots_of(route_t, PART, 2, part * PART)
        spread = jnp.where(mask, weight[:, None, :], 0.0).reshape(2 * EXPERTS * PART, rows).T
        high = spread.astype(BF16)
        out_ref[part, 0:rows, :] = high
        out_ref[part, rows : 2 * rows, :] = (spread - high.astype(F32)).astype(BF16)


def mixing(route_t, weight_t, rows):
    vmem = pl.BlockSpec(memory_space=pltpu.VMEM)
    return pl.pallas_call(
        functools.partial(mixing_body, rows),
        in_specs=[vmem, vmem],
        out_specs=vmem,
        out_shape=jax.ShapeDtypeStruct((CAP // PART, 2 * rows, 2 * EXPERTS * PART), BF16),
        cost_estimate=pl.CostEstimate(flops=1 << 20, bytes_accessed=1 << 17, transcendentals=0),
        name="mixing",
    )(route_t, weight_t)


def ffn_body(
    place_ref, x_ref, wg_ref, wu_ref, wd_ref, own_ref, far_ref, out_ref,
    gate_ref, up_ref, low_ref, right_ref, hidden_ref, mid_ref, outr_ref,
):
    step = pl.program_id(0)
    group, half = place_ref[0], place_ref[1]
    width = hidden_ref.shape[1]
    span = x_ref.shape[1]
    packs = (own_ref, far_ref)

    for turn in range(4):

        @pl.when(step == turn)
        def _(turn=turn):
            xh, pack = turn // 2, packs[turn % 2]
            there = group ^ turn
            near, across = ROWS_AT[xh]
            x = x_ref[...]
            left = jnp.concatenate(
                [
                    pack[near : near + 32, 0:span],
                    pack[near : near + 32, span : 2 * span],
                    pack[across : across + 32, 0:span],
                    pack[across : across + 32, span : 2 * span],
                ],
                axis=0,
            )
            gate = jnp.dot(x, wg_ref[...], preferred_element_type=F32)
            up = jnp.dot(x, wu_ref[...], preferred_element_type=F32)
            low = lax.dot_general(x, left, NT, preferred_element_type=F32)
            if turn == 0:
                right_ref[...] = jnp.zeros_like(right_ref)
            else:
                gate += gate_ref[...]
                up += up_ref[...]
                low += low_ref[...]
            ranks = (half ^ (there >> 1)) * 64 + (there & 1) * 16
            r0 = pl.multiple_of(ranks, 16)
            r1 = pl.multiple_of(ranks + 32, 16)
            right_ref[pl.ds(r0, 16), 0:width] = pack[near + 48 : near + 64, 0:width]
            right_ref[pl.ds(r1, 16), width : 2 * width] = pack[
                near + 48 : near + 64, width : 2 * width
            ]
            cols = outr_ref.shape[2]
            outr_ref[0, turn * 16 : turn * 16 + 16, :] = pack[near + 32 : near + 48, 0:cols]
            outr_ref[1, turn * 16 : turn * 16 + 16, :] = pack[across + 32 : across + 48, 0:cols]
            if turn < 3:
                gate_ref[...], up_ref[...], low_ref[...] = gate, up, low
                return
            scaled = (ADAPTER_SCALE * low).astype(BF16)
            gate += jnp.dot(scaled, right_ref[:, 0:width], preferred_element_type=F32)
            up += jnp.dot(scaled, right_ref[:, width : 2 * width], preferred_element_type=F32)
            hidden = (jax.nn.silu(gate) * up).astype(BF16)
            hidden_ref[...] = hidden
            left = jnp.concatenate(
                [
                    packs[t % 2][
                        ROWS_AT[t // 2][0] + 48 : ROWS_AT[t // 2][0] + 64, 2 * width : 3 * width
                    ]
                    for t in range(4)
                ],
                axis=0,
            )
            mid = lax.dot_general(hidden, left, NT, preferred_element_type=F32)
            mid_ref[...] = (ADAPTER_SCALE * mid).astype(BF16)

    @pl.when(step >= 4)
    def _():
        cols = out_ref.shape[1]
        start = (step - 4) * cols
        side = start // outr_ref.shape[2]
        offset = pl.multiple_of(start - side * outr_ref.shape[2], cols)
        out = jnp.dot(hidden_ref[...], wd_ref[...], preferred_element_type=F32)
        out += jnp.dot(
            mid_ref[...], outr_ref[half ^ side, :, pl.ds(offset, cols)], preferred_element_type=F32
        )
        out_ref[...] = out.astype(BF16)


def feed_forward(place, x, wg, wu, wd, own, far, limit):
    rows, width = x.shape
    hidden = wg.shape[1]
    span, cols = width // 4, 1024
    turn = lambda i, s: s[0] ^ jnp.minimum(i, 3)
    later = lambda i: jnp.maximum(i - 4, 0)
    whole = lambda a: pl.BlockSpec(a.shape, lambda i, s: (0,) * a.ndim)
    return pl.pallas_call(
        ffn_body,
        grid_spec=pltpu.PrefetchScalarGridSpec(
            num_scalar_prefetch=1,
            grid=(4 + width // cols,),
            in_specs=[
                pl.BlockSpec((rows, span), lambda i, s: (0, turn(i, s))),
                pl.BlockSpec((span, hidden), lambda i, s: (turn(i, s), 0)),
                pl.BlockSpec((span, hidden), lambda i, s: (turn(i, s), 0)),
                pl.BlockSpec((hidden, cols), lambda i, s: (0, later(i))),
                whole(own),
                whole(far),
            ],
            out_specs=pl.BlockSpec((rows, cols), lambda i, s: (0, later(i))),
            scratch_shapes=[
                pltpu.VMEM((rows, hidden), F32),
                pltpu.VMEM((rows, hidden), F32),
                pltpu.VMEM((rows, 128), F32),
                pltpu.VMEM((128, 2 * hidden), BF16),
                pltpu.VMEM((rows, hidden), BF16),
                pltpu.VMEM((rows, 64), BF16),
                pltpu.VMEM((2, 64, width // 2), BF16),
            ],
        ),
        out_shape=pltpu.HBM((rows, width), BF16),
        compiler_params=pltpu.CompilerParams(vmem_limit_bytes=limit),
        cost_estimate=pl.CostEstimate(
            flops=6 * rows * width * hidden, bytes_accessed=28 << 20, transcendentals=rows * hidden
        ),
        name="feed_forward",
    )(place, x, wg, wu, wd, own, far)


def combine_body(mix_ref, part_ref, *refs):
    out_ref = refs[-1]
    rows = out_ref.shape[0]
    both = jnp.dot(mix_ref[...], part_ref[...], preferred_element_type=F32)
    total = both[0:rows] + both[rows : 2 * rows]
    if len(refs) == 2:
        total += refs[0][...]
    out_ref[...] = total.astype(out_ref.dtype)


def combine(mix, part, base, out_type):
    slots, width = part.shape
    rows = mix.shape[0] // 2
    cols = width
    sheet = pl.BlockSpec((rows, cols), lambda i: (0, i))
    in_specs = [
        pl.BlockSpec(mix.shape, lambda i: (0, 0)),
        pl.BlockSpec((slots, cols), lambda i: (0, i)),
    ]
    operands = (mix, part)
    if base is not None:
        in_specs.append(sheet)
        operands += (base,)
    return pl.pallas_call(
        combine_body,
        grid=(width // cols,),
        out_shape=jax.ShapeDtypeStruct((rows, width), out_type),
        in_specs=in_specs,
        out_specs=sheet,
        compiler_params=pltpu.CompilerParams(vmem_limit_bytes=32 << 20),
        cost_estimate=pl.CostEstimate(
            flops=4 * slots * rows * width, bytes_accessed=3 << 20, transcendentals=0
        ),
        name="combine",
    )(*operands)


def stack(pieces):
    rows, total, at = sum(piece.shape[0] for piece in pieces), None, 0
    for piece in pieces:
        after = rows - at - piece.shape[0]
        padded = jnp.pad(piece, ((at, after), (0, 0)))
        total = padded if total is None else total + padded
        at += piece.shape[0]
    return total


def gather_factors(input_left, input_right, output_left, output_right):
    left = jnp.transpose(input_left, (2, 0, 1)).reshape(input_left.shape[2], -1)
    right = jnp.concatenate([input_right[0], input_right[1], output_left.T], axis=1)
    wide = right.shape[1]
    pad = lambda a: jnp.pad(a, ((0, 0), (0, wide - a.shape[1])))
    mine = jnp.concatenate([pad(left), pad(output_right), right], axis=0)
    shared = left.shape[0] + output_right.shape[0]
    groups, tensor = lax.axis_size("group"), lax.axis_size("tensor")
    both = [
        (g * tensor + t, (g ^ 2) * tensor + (t ^ 1)) for g in range(groups) for t in range(tensor)
    ]
    across_x = exchange(mine, "group", 2)
    partner = exchange(mine[:shared], "tensor", 1)
    corner = lax.ppermute(mine[:shared], ("group", "tensor"), both)
    return mine, across_x, partner, corner


def on_device(
    tokens,
    expert_norm_gain,
    routing,
    chosen_expert_weights,
    resident_gate_weight,
    resident_up_weight,
    resident_down_weight,
    adapter_input_left,
    adapter_input_right,
    adapter_output_left,
    adapter_output_right,
):
    rows, width = tokens.shape
    position = lax.axis_index("tensor")
    place = jnp.stack([lax.axis_index("group"), position % 2]).astype(jnp.int32)
    pieces = gather_factors(
        adapter_input_left, adapter_input_right, adapter_output_left, adapter_output_right
    )
    route_t, gain = routing.T, expert_norm_gain.reshape(1, width)
    sent = [dispatch(tokens, gain, route_t, first) for first in range(0, CAP, PART)]
    mix = mixing(route_t, chosen_expert_weights.T, rows)

    def travel(value):
        value = value.reshape(2 * EXPERTS, PART, width)
        return lax.all_to_all(value, "tensor", 0, 0, tiled=True).reshape(-1, width)

    weights = (resident_gate_weight, resident_up_weight, resident_down_weight)
    arrived = [travel(value) for value in sent]
    *pieces, arrived[0] = lax.optimization_barrier((*pieces, arrived[0]))
    own = stack(pieces)
    far = exchange(own, "group", 1)
    parts = [
        travel(feed_forward(place, x, *weights, own, far, limit))
        for x, limit in zip(arrived, FFN_VMEM)
    ]
    base = combine(mix[0], parts[0], None, F32)
    return combine(mix[1], parts[1], base, BF16)


def solution(mesh):
    return jax.shard_map(
        on_device,
        mesh=mesh,
        in_specs=(
            P(("group", "tensor"), None),
            P(),
            P("group", None),
            P("group", None),
            P(None, "tensor"),
            P(None, "tensor"),
            P("tensor", None),
            P(None, "group", "tensor"),
            P(None, "group", "tensor"),
            P("tensor", "group"),
            P("group", "tensor"),
        ),
        out_specs=P(("group", "tensor"), None),
        check_vma=False,
    )
```

```python
import functools

import jax
import jax.numpy as jnp
from jax import lax
from jax.experimental import pallas as pl
from jax.experimental.pallas import tpu as pltpu
from jax.sharding import PartitionSpec as P

ADAPTER_SCALE = 0.5
NORM_EPS = 1e-06
EXPERTS = 16
CAP = 16
PART = CAP // 2
FFN_VMEM = (50 << 20, 62 << 20)
ROWS_AT = ((0, 128), (64, 176))
DISPATCH_VMEM = 64 << 20
F32 = jnp.float32
BF16 = jnp.bfloat16
NT = (((1,), (1,)), ((), ()))
TN = (((0,), (0,)), ((), ()))


def exchange(value, axis, bit):
    return lax.ppermute(value, axis, [(i, i ^ bit) for i in range(lax.axis_size(axis))])


def own_rows(table_ref, rows):
    position = lax.axis_index("tensor")
    per = 128 // rows
    start = pl.multiple_of((position // per) * 128, 128)
    block = table_ref[:, pl.ds(start, 128)]
    return pltpu.roll(block, (128 - (position % per) * rows) % 128, 1)[:, 0:rows]


def slots_of(route_t, depth, copies, first):
    rows = route_t.shape[1]
    experts = lax.broadcasted_iota(jnp.int32, (EXPERTS, rows), 0)
    chosen = jnp.zeros((EXPERTS, rows), jnp.bool_)
    for k in range(route_t.shape[0]):
        chosen = chosen | (route_t[k : k + 1, :] == experts)
    upper = (
        lax.broadcasted_iota(jnp.int32, (rows, rows), 0)
        <= lax.broadcasted_iota(jnp.int32, (rows, rows), 1)
    ).astype(F32)
    place = jnp.dot(chosen.astype(F32), upper, preferred_element_type=F32).astype(jnp.int32) - 1
    place = jnp.where(chosen, place, -1)
    slot = lax.broadcasted_iota(jnp.int32, (EXPERTS, copies * depth, rows), 1) % depth
    return place[:, None, :] == slot + first


def dispatch_body(first, tokens_ref, gain_ref, route_ref, out_ref, normed_ref, mask_ref):
    step = pl.program_id(0)

    @pl.when(step == 0)
    def _():
        wide = tokens_ref[...].astype(F32)
        spread = jnp.mean(wide * wide, axis=-1, keepdims=True)
        normed_ref[...] = (wide * lax.rsqrt(spread + NORM_EPS) * gain_ref[...]).astype(BF16)
        mask = slots_of(own_rows(route_ref, tokens_ref.shape[0]), PART, 1, first)
        mask_ref[...] = mask.astype(F32).reshape(EXPERTS * PART, -1).astype(BF16)

    per = out_ref.shape[0]
    pick = mask_ref[pl.ds(pl.multiple_of(step * per * PART, per * PART), per * PART), :]
    rows = jnp.dot(pick, normed_ref[...], preferred_element_type=F32)
    for i in range(per):
        for half in range(2):
            out_ref[i, half] = rows[i * PART : (i + 1) * PART].astype(BF16)


def dispatch(tokens, gain, route_t, first):
    rows, width = tokens.shape
    steps = 2
    per = EXPERTS // steps
    return pl.pallas_call(
        functools.partial(dispatch_body, first),
        grid=(steps,),
        out_shape=pltpu.HBM((EXPERTS, 2, PART, width), BF16),
        in_specs=[
            pl.BlockSpec((rows, width), lambda i: (0, 0)),
            pl.BlockSpec((1, width), lambda i: (0, 0)),
            pl.BlockSpec(route_t.shape, lambda i: (0, 0)),
        ],
        out_specs=pl.BlockSpec((per, 2, PART, width), lambda i: (i, 0, 0, 0)),
        scratch_shapes=[pltpu.VMEM((rows, width), BF16), pltpu.VMEM((EXPERTS * PART, rows), BF16)],
        compiler_params=pltpu.CompilerParams(vmem_limit_bytes=DISPATCH_VMEM),
        cost_estimate=pl.CostEstimate(
            flops=2 * EXPERTS * PART * rows * width, bytes_accessed=3 << 20, transcendentals=0
        ),
        name="dispatch",
    )(tokens, gain, route_t)


def mixing_body(rows, route_ref, weight_ref, out_ref):
    route_t, weight_t = own_rows(route_ref, rows), own_rows(weight_ref, rows)
    experts = lax.broadcasted_iota(jnp.int32, (EXPERTS, rows), 0)
    weight = jnp.zeros((EXPERTS, rows), F32)
    for k in range(route_t.shape[0]):
        weight += jnp.where(route_t[k : k + 1, :] == experts, weight_t[k : k + 1, :], 0.0)
    for part in range(CAP // PART):
        mask = slots_of(route_t, PART, 2, part * PART)
        spread = jnp.where(mask, weight[:, None, :], 0.0).reshape(2 * EXPERTS * PART, rows).T
        high = spread.astype(BF16)
        out_ref[part, 0:rows, :] = high
        out_ref[part, rows : 2 * rows, :] = (spread - high.astype(F32)).astype(BF16)


def mixing(route_t, weight_t, rows):
    vmem = pl.BlockSpec(memory_space=pltpu.VMEM)
    return pl.pallas_call(
        functools.partial(mixing_body, rows),
        in_specs=[vmem, vmem],
        out_specs=vmem,
        out_shape=jax.ShapeDtypeStruct((CAP // PART, 2 * rows, 2 * EXPERTS * PART), BF16),
        cost_estimate=pl.CostEstimate(flops=1 << 20, bytes_accessed=1 << 17, transcendentals=0),
        name="mixing",
    )(route_t, weight_t)


def ffn_body(
    place_ref, x_ref, wg_ref, wu_ref, wd_ref, own_ref, far_ref, out_ref,
    gate_ref, up_ref, low_ref, right_ref, hidden_ref, mid_ref, outr_ref,
):
    step = pl.program_id(0)
    group, half = place_ref[0], place_ref[1]
    width = hidden_ref.shape[1]
    span = x_ref.shape[1]
    packs = (own_ref, far_ref)

    for turn in range(4):

        @pl.when(step == turn)
        def _(turn=turn):
            xh, pack = turn // 2, packs[turn % 2]
            there = group ^ turn
            near, across = ROWS_AT[xh]
            x = x_ref[...]
            left = jnp.concatenate(
                [
                    pack[near : near + 32, 0:span],
                    pack[near : near + 32, span : 2 * span],
                    pack[across : across + 32, 0:span],
                    pack[across : across + 32, span : 2 * span],
                ],
                axis=0,
            )
            gate = jnp.dot(x, wg_ref[...], preferred_element_type=F32)
            up = jnp.dot(x, wu_ref[...], preferred_element_type=F32)
            low = lax.dot_general(x, left, NT, preferred_element_type=F32)
            if turn == 0:
                right_ref[...] = jnp.zeros_like(right_ref)
            else:
                gate += gate_ref[...]
                up += up_ref[...]
                low += low_ref[...]
            ranks = (half ^ (there >> 1)) * 64 + (there & 1) * 16
            r0 = pl.multiple_of(ranks, 16)
            r1 = pl.multiple_of(ranks + 32, 16)
            right_ref[pl.ds(r0, 16), 0:width] = pack[near + 48 : near + 64, 0:width]
            right_ref[pl.ds(r1, 16), width : 2 * width] = pack[
                near + 48 : near + 64, width : 2 * width
            ]
            cols = outr_ref.shape[2]
            outr_ref[0, turn * 16 : turn * 16 + 16, :] = pack[near + 32 : near + 48, 0:cols]
            outr_ref[1, turn * 16 : turn * 16 + 16, :] = pack[across + 32 : across + 48, 0:cols]
            if turn < 3:
                gate_ref[...], up_ref[...], low_ref[...] = gate, up, low
                return
            scaled = (ADAPTER_SCALE * low).astype(BF16)
            gate += jnp.dot(scaled, right_ref[:, 0:width], preferred_element_type=F32)
            up += jnp.dot(scaled, right_ref[:, width : 2 * width], preferred_element_type=F32)
            hidden = (jax.nn.silu(gate) * up).astype(BF16)
            hidden_ref[...] = hidden
            left = jnp.concatenate(
                [
                    packs[t % 2][
                        ROWS_AT[t // 2][0] + 48 : ROWS_AT[t // 2][0] + 64, 2 * width : 3 * width
                    ]
                    for t in range(4)
                ],
                axis=0,
            )
            mid = lax.dot_general(hidden, left, NT, preferred_element_type=F32)
            mid_ref[...] = (ADAPTER_SCALE * mid).astype(BF16)

    @pl.when(step >= 4)
    def _():
        cols = out_ref.shape[1]
        start = (step - 4) * cols
        side = start // outr_ref.shape[2]
        offset = pl.multiple_of(start - side * outr_ref.shape[2], cols)
        out = jnp.dot(hidden_ref[...], wd_ref[...], preferred_element_type=F32)
        out += jnp.dot(
            mid_ref[...], outr_ref[half ^ side, :, pl.ds(offset, cols)], preferred_element_type=F32
        )
        out_ref[...] = out.astype(BF16)


def feed_forward(place, x, wg, wu, wd, own, far, limit):
    rows, width = x.shape
    hidden = wg.shape[1]
    span, cols = width // 4, 1024
    turn = lambda i, s: s[0] ^ jnp.minimum(i, 3)
    later = lambda i: jnp.maximum(i - 4, 0)
    whole = lambda a: pl.BlockSpec(a.shape, lambda i, s: (0,) * a.ndim)
    return pl.pallas_call(
        ffn_body,
        grid_spec=pltpu.PrefetchScalarGridSpec(
            num_scalar_prefetch=1,
            grid=(4 + width // cols,),
            in_specs=[
                pl.BlockSpec((rows, span), lambda i, s: (0, turn(i, s))),
                pl.BlockSpec((span, hidden), lambda i, s: (turn(i, s), 0)),
                pl.BlockSpec((span, hidden), lambda i, s: (turn(i, s), 0)),
                pl.BlockSpec((hidden, cols), lambda i, s: (0, later(i))),
                whole(own),
                whole(far),
            ],
            out_specs=pl.BlockSpec((rows, cols), lambda i, s: (0, later(i))),
            scratch_shapes=[
                pltpu.VMEM((rows, hidden), F32),
                pltpu.VMEM((rows, hidden), F32),
                pltpu.VMEM((rows, 128), F32),
                pltpu.VMEM((128, 2 * hidden), BF16),
                pltpu.VMEM((rows, hidden), BF16),
                pltpu.VMEM((rows, 64), BF16),
                pltpu.VMEM((2, 64, width // 2), BF16),
            ],
        ),
        out_shape=pltpu.HBM((rows, width), BF16),
        compiler_params=pltpu.CompilerParams(vmem_limit_bytes=limit),
        cost_estimate=pl.CostEstimate(
            flops=6 * rows * width * hidden, bytes_accessed=28 << 20, transcendentals=rows * hidden
        ),
        name="feed_forward",
    )(place, x, wg, wu, wd, own, far)


def combine_body(mix_ref, part_ref, *refs):
    out_ref = refs[-1]
    rows = out_ref.shape[0]
    both = jnp.dot(mix_ref[...], part_ref[...], preferred_element_type=F32)
    total = both[0:rows] + both[rows : 2 * rows]
    if len(refs) == 2:
        total += refs[0][...]
    out_ref[...] = total.astype(out_ref.dtype)


def combine(mix, part, base, out_type):
    slots, width = part.shape
    rows = mix.shape[0] // 2
    cols = width
    sheet = pl.BlockSpec((rows, cols), lambda i: (0, i))
    in_specs = [
        pl.BlockSpec(mix.shape, lambda i: (0, 0)),
        pl.BlockSpec((slots, cols), lambda i: (0, i)),
    ]
    operands = (mix, part)
    if base is not None:
        in_specs.append(sheet)
        operands += (base,)
    return pl.pallas_call(
        combine_body,
        grid=(width // cols,),
        out_shape=jax.ShapeDtypeStruct((rows, width), out_type),
        in_specs=in_specs,
        out_specs=sheet,
        compiler_params=pltpu.CompilerParams(vmem_limit_bytes=32 << 20),
        cost_estimate=pl.CostEstimate(
            flops=4 * slots * rows * width, bytes_accessed=3 << 20, transcendentals=0
        ),
        name="combine",
    )(*operands)


def stack(pieces):
    rows, total, at = sum(piece.shape[0] for piece in pieces), None, 0
    wide = max(piece.shape[1] for piece in pieces)
    for piece in pieces:
        after = rows - at - piece.shape[0]
        padded = jnp.pad(piece, ((at, after), (0, wide - piece.shape[1])))
        total = padded if total is None else total + padded
        at += piece.shape[0]
    return total


def gather_factors(input_left, input_right, output_left, output_right):
    left = jnp.transpose(input_left, (2, 0, 1)).reshape(input_left.shape[2], -1)
    right = jnp.concatenate([input_right[0], input_right[1], output_left.T], axis=1)
    wide = right.shape[1]
    pad = lambda a: jnp.pad(a, ((0, 0), (0, wide - a.shape[1])))
    mine = jnp.concatenate([pad(left), pad(output_right), right], axis=0)
    groups, tensor = lax.axis_size("group"), lax.axis_size("tensor")
    both = [
        (g * tensor + t, (g ^ 2) * tensor + (t ^ 1)) for g in range(groups) for t in range(tensor)
    ]
    across_x = exchange(mine, "group", 2)
    pair = jnp.concatenate([left, output_right], axis=0)
    partner = exchange(pair, "tensor", 1)
    corner = lax.ppermute(pair, ("group", "tensor"), both)
    return mine, across_x, partner, corner


def on_device(
    tokens,
    expert_norm_gain,
    routing,
    chosen_expert_weights,
    resident_gate_weight,
    resident_up_weight,
    resident_down_weight,
    adapter_input_left,
    adapter_input_right,
    adapter_output_left,
    adapter_output_right,
):
    rows, width = tokens.shape
    position = lax.axis_index("tensor")
    place = jnp.stack([lax.axis_index("group"), position % 2]).astype(jnp.int32)
    pieces = gather_factors(
        adapter_input_left, adapter_input_right, adapter_output_left, adapter_output_right
    )
    route_t, gain = routing.T, expert_norm_gain.reshape(1, width)
    sent = [dispatch(tokens, gain, route_t, first) for first in range(0, CAP, PART)]
    mix = mixing(route_t, chosen_expert_weights.T, rows)

    def travel(value):
        value = value.reshape(2 * EXPERTS, PART, width)
        return lax.all_to_all(value, "tensor", 0, 0, tiled=True).reshape(-1, width)

    weights = (resident_gate_weight, resident_up_weight, resident_down_weight)
    arrived = [travel(value) for value in sent]
    *pieces, arrived[0] = lax.optimization_barrier((*pieces, arrived[0]))
    own = stack(pieces)
    far = exchange(own, "group", 1)
    parts = [
        travel(feed_forward(place, x, *weights, own, far, limit))
        for x, limit in zip(arrived, FFN_VMEM)
    ]
    base = combine(mix[0], parts[0], None, F32)
    return combine(mix[1], parts[1], base, BF16)


def solution(mesh):
    return jax.shard_map(
        on_device,
        mesh=mesh,
        in_specs=(
            P(("group", "tensor"), None),
            P(),
            P("group", None),
            P("group", None),
            P(None, "tensor"),
            P(None, "tensor"),
            P("tensor", None),
            P(None, "group", "tensor"),
            P(None, "group", "tensor"),
            P("tensor", "group"),
            P("group", "tensor"),
        ),
        out_specs=P(("group", "tensor"), None),
        check_vma=False,
    )
```

```python
import functools

import jax
import jax.numpy as jnp
from jax import lax
from jax.experimental import pallas as pl
from jax.experimental.pallas import tpu as pltpu
from jax.sharding import PartitionSpec as P

ADAPTER_SCALE = 0.5
NORM_EPS = 1e-06
EXPERTS = 16
CAP = 16
PART = CAP // 2
FFN_VMEM = (50 << 20, 62 << 20)
ROWS_AT = ((0, 128), (64, 176))
DISPATCH_VMEM = 64 << 20
F32 = jnp.float32
BF16 = jnp.bfloat16
NT = (((1,), (1,)), ((), ()))
TN = (((0,), (0,)), ((), ()))


def exchange(value, axis, bit):
    return lax.ppermute(value, axis, [(i, i ^ bit) for i in range(lax.axis_size(axis))])


def own_rows(table_ref, rows):
    position = lax.axis_index("tensor")
    per = 128 // rows
    start = pl.multiple_of((position // per) * 128, 128)
    block = table_ref[:, pl.ds(start, 128)]
    return pltpu.roll(block, (128 - (position % per) * rows) % 128, 1)[:, 0:rows]


def slots_of(route_t, depth, copies, first):
    rows = route_t.shape[1]
    experts = lax.broadcasted_iota(jnp.int32, (EXPERTS, rows), 0)
    chosen = jnp.zeros((EXPERTS, rows), jnp.bool_)
    for k in range(route_t.shape[0]):
        chosen = chosen | (route_t[k : k + 1, :] == experts)
    upper = (
        lax.broadcasted_iota(jnp.int32, (rows, rows), 0)
        <= lax.broadcasted_iota(jnp.int32, (rows, rows), 1)
    ).astype(F32)
    place = jnp.dot(chosen.astype(F32), upper, preferred_element_type=F32).astype(jnp.int32) - 1
    place = jnp.where(chosen, place, -1)
    slot = lax.broadcasted_iota(jnp.int32, (EXPERTS, copies * depth, rows), 1) % depth
    return place[:, None, :] == slot + first


def dispatch_body(first, tokens_ref, gain_ref, route_ref, out_ref, normed_ref, mask_ref):
    step = pl.program_id(0)

    @pl.when(step == 0)
    def _():
        wide = tokens_ref[...].astype(F32)
        spread = jnp.mean(wide * wide, axis=-1, keepdims=True)
        normed_ref[...] = (wide * lax.rsqrt(spread + NORM_EPS) * gain_ref[...]).astype(BF16)
        mask = slots_of(own_rows(route_ref, tokens_ref.shape[0]), PART, 1, first)
        mask_ref[...] = mask.astype(F32).reshape(EXPERTS * PART, -1).astype(BF16)

    per = out_ref.shape[0]
    pick = mask_ref[pl.ds(pl.multiple_of(step * per * PART, per * PART), per * PART), :]
    rows = jnp.dot(pick, normed_ref[...], preferred_element_type=F32)
    rows = rows.reshape(per, 1, PART, rows.shape[1]).astype(BF16)
    out_ref[...] = jnp.broadcast_to(rows, out_ref.shape)


def dispatch(tokens, gain, route_t, first):
    rows, width = tokens.shape
    steps = 2
    per = EXPERTS // steps
    return pl.pallas_call(
        functools.partial(dispatch_body, first),
        grid=(steps,),
        out_shape=pltpu.HBM((EXPERTS, 2, PART, width), BF16),
        in_specs=[
            pl.BlockSpec((rows, width), lambda i: (0, 0)),
            pl.BlockSpec((1, width), lambda i: (0, 0)),
            pl.BlockSpec(route_t.shape, lambda i: (0, 0)),
        ],
        out_specs=pl.BlockSpec((per, 2, PART, width), lambda i: (i, 0, 0, 0)),
        scratch_shapes=[pltpu.VMEM((rows, width), BF16), pltpu.VMEM((EXPERTS * PART, rows), BF16)],
        compiler_params=pltpu.CompilerParams(vmem_limit_bytes=DISPATCH_VMEM),
        cost_estimate=pl.CostEstimate(
            flops=2 * EXPERTS * PART * rows * width, bytes_accessed=3 << 20, transcendentals=0
        ),
        name="dispatch",
    )(tokens, gain, route_t)


def mixing_body(rows, route_ref, weight_ref, out_ref):
    route_t, weight_t = own_rows(route_ref, rows), own_rows(weight_ref, rows)
    experts = lax.broadcasted_iota(jnp.int32, (EXPERTS, rows), 0)
    weight = jnp.zeros((EXPERTS, rows), F32)
    for k in range(route_t.shape[0]):
        weight += jnp.where(route_t[k : k + 1, :] == experts, weight_t[k : k + 1, :], 0.0)
    for part in range(CAP // PART):
        mask = slots_of(route_t, PART, 2, part * PART)
        spread = jnp.where(mask, weight[:, None, :], 0.0).reshape(2 * EXPERTS * PART, rows).T
        high = spread.astype(BF16)
        out_ref[part, 0:rows, :] = high
        out_ref[part, rows : 2 * rows, :] = (spread - high.astype(F32)).astype(BF16)


def mixing(route_t, weight_t, rows):
    vmem = pl.BlockSpec(memory_space=pltpu.VMEM)
    return pl.pallas_call(
        functools.partial(mixing_body, rows),
        in_specs=[vmem, vmem],
        out_specs=vmem,
        out_shape=jax.ShapeDtypeStruct((CAP // PART, 2 * rows, 2 * EXPERTS * PART), BF16),
        cost_estimate=pl.CostEstimate(flops=1 << 20, bytes_accessed=1 << 17, transcendentals=0),
        name="mixing",
    )(route_t, weight_t)


def ffn_body(
    place_ref, x_ref, wg_ref, wu_ref, wd_ref, own_ref, far_ref, out_ref,
    gate_ref, up_ref, low_ref, right_ref, hidden_ref, mid_ref, outr_ref,
):
    step = pl.program_id(0)
    group, half = place_ref[0], place_ref[1]
    width = hidden_ref.shape[1]
    span = x_ref.shape[1]
    packs = (own_ref, far_ref)

    for turn in range(4):

        @pl.when(step == turn)
        def _(turn=turn):
            xh, pack = turn // 2, packs[turn % 2]
            there = group ^ turn
            near, across = ROWS_AT[xh]
            x = x_ref[...]
            left = jnp.concatenate(
                [
                    pack[near : near + 32, 0:span],
                    pack[near : near + 32, span : 2 * span],
                    pack[across : across + 32, 0:span],
                    pack[across : across + 32, span : 2 * span],
                ],
                axis=0,
            )
            gate = jnp.dot(x, wg_ref[...], preferred_element_type=F32)
            up = jnp.dot(x, wu_ref[...], preferred_element_type=F32)
            low = lax.dot_general(x, left, NT, preferred_element_type=F32)
            if turn == 0:
                right_ref[...] = jnp.zeros_like(right_ref)
            else:
                gate += gate_ref[...]
                up += up_ref[...]
                low += low_ref[...]
            ranks = (half ^ (there >> 1)) * 64 + (there & 1) * 16
            r0 = pl.multiple_of(ranks, 16)
            r1 = pl.multiple_of(ranks + 32, 16)
            right_ref[pl.ds(r0, 16), 0:width] = pack[near + 48 : near + 64, 0:width]
            right_ref[pl.ds(r1, 16), width : 2 * width] = pack[
                near + 48 : near + 64, width : 2 * width
            ]
            cols = outr_ref.shape[2]
            outr_ref[0, turn * 16 : turn * 16 + 16, :] = pack[near + 32 : near + 48, 0:cols]
            outr_ref[1, turn * 16 : turn * 16 + 16, :] = pack[across + 32 : across + 48, 0:cols]
            if turn < 3:
                gate_ref[...], up_ref[...], low_ref[...] = gate, up, low
                return
            scaled = (ADAPTER_SCALE * low).astype(BF16)
            gate += jnp.dot(scaled, right_ref[:, 0:width], preferred_element_type=F32)
            up += jnp.dot(scaled, right_ref[:, width : 2 * width], preferred_element_type=F32)
            hidden = (jax.nn.silu(gate) * up).astype(BF16)
            hidden_ref[...] = hidden
            left = jnp.concatenate(
                [
                    packs[t % 2][
                        ROWS_AT[t // 2][0] + 48 : ROWS_AT[t // 2][0] + 64, 2 * width : 3 * width
                    ]
                    for t in range(4)
                ],
                axis=0,
            )
            mid = lax.dot_general(hidden, left, NT, preferred_element_type=F32)
            mid_ref[...] = (ADAPTER_SCALE * mid).astype(BF16)

    @pl.when(step >= 4)
    def _():
        cols = out_ref.shape[1]
        start = (step - 4) * cols
        side = start // outr_ref.shape[2]
        offset = pl.multiple_of(start - side * outr_ref.shape[2], cols)
        out = jnp.dot(hidden_ref[...], wd_ref[...], preferred_element_type=F32)
        out += jnp.dot(
            mid_ref[...], outr_ref[half ^ side, :, pl.ds(offset, cols)], preferred_element_type=F32
        )
        out_ref[...] = out.astype(BF16)


def feed_forward(place, x, wg, wu, wd, own, far, limit):
    rows, width = x.shape
    hidden = wg.shape[1]
    span, cols = width // 4, 2048
    turn = lambda i, s: s[0] ^ jnp.minimum(i, 3)
    later = lambda i: jnp.maximum(i - 4, 0)
    whole = lambda a: pl.BlockSpec(a.shape, lambda i, s: (0,) * a.ndim)
    return pl.pallas_call(
        ffn_body,
        grid_spec=pltpu.PrefetchScalarGridSpec(
            num_scalar_prefetch=1,
            grid=(4 + width // cols,),
            in_specs=[
                pl.BlockSpec((rows, span), lambda i, s: (0, turn(i, s))),
                pl.BlockSpec((span, hidden), lambda i, s: (turn(i, s), 0)),
                pl.BlockSpec((span, hidden), lambda i, s: (turn(i, s), 0)),
                pl.BlockSpec((hidden, cols), lambda i, s: (0, later(i))),
                whole(own),
                whole(far),
            ],
            out_specs=pl.BlockSpec((rows, cols), lambda i, s: (0, later(i))),
            scratch_shapes=[
                pltpu.VMEM((rows, hidden), F32),
                pltpu.VMEM((rows, hidden), F32),
                pltpu.VMEM((rows, 128), F32),
                pltpu.VMEM((128, 2 * hidden), BF16),
                pltpu.VMEM((rows, hidden), BF16),
                pltpu.VMEM((rows, 64), BF16),
                pltpu.VMEM((2, 64, width // 2), BF16),
            ],
        ),
        out_shape=pltpu.HBM((rows, width), BF16),
        compiler_params=pltpu.CompilerParams(vmem_limit_bytes=limit),
        cost_estimate=pl.CostEstimate(
            flops=6 * rows * width * hidden, bytes_accessed=28 << 20, transcendentals=rows * hidden
        ),
        name="feed_forward",
    )(place, x, wg, wu, wd, own, far)


def combine_body(mix_ref, part_ref, *refs):
    out_ref = refs[-1]
    rows = out_ref.shape[0]
    both = jnp.dot(mix_ref[...], part_ref[...], preferred_element_type=F32)
    total = both[0:rows] + both[rows : 2 * rows]
    if len(refs) == 2:
        total += refs[0][...]
    out_ref[...] = total.astype(out_ref.dtype)


def combine(mix, part, base, out_type):
    slots, width = part.shape
    rows = mix.shape[0] // 2
    cols = width
    sheet = pl.BlockSpec((rows, cols), lambda i: (0, i))
    in_specs = [
        pl.BlockSpec(mix.shape, lambda i: (0, 0)),
        pl.BlockSpec((slots, cols), lambda i: (0, i)),
    ]
    operands = (mix, part)
    if base is not None:
        in_specs.append(sheet)
        operands += (base,)
    return pl.pallas_call(
        combine_body,
        grid=(width // cols,),
        out_shape=jax.ShapeDtypeStruct((rows, width), out_type),
        in_specs=in_specs,
        out_specs=sheet,
        compiler_params=pltpu.CompilerParams(vmem_limit_bytes=32 << 20),
        cost_estimate=pl.CostEstimate(
            flops=4 * slots * rows * width, bytes_accessed=3 << 20, transcendentals=0
        ),
        name="combine",
    )(*operands)


def stack(pieces):
    rows, total, at = sum(piece.shape[0] for piece in pieces), None, 0
    wide = max(piece.shape[1] for piece in pieces)
    for piece in pieces:
        after = rows - at - piece.shape[0]
        padded = jnp.pad(piece, ((at, after), (0, wide - piece.shape[1])))
        total = padded if total is None else total + padded
        at += piece.shape[0]
    return total


def gather_factors(input_left, input_right, output_left, output_right):
    left = jnp.transpose(input_left, (2, 0, 1)).reshape(input_left.shape[2], -1)
    right = jnp.concatenate([input_right[0], input_right[1], output_left.T], axis=1)
    wide = right.shape[1]
    pad = lambda a: jnp.pad(a, ((0, 0), (0, wide - a.shape[1])))
    mine = jnp.concatenate([pad(left), pad(output_right), right], axis=0)
    groups, tensor = lax.axis_size("group"), lax.axis_size("tensor")
    both = [
        (g * tensor + t, (g ^ 2) * tensor + (t ^ 1)) for g in range(groups) for t in range(tensor)
    ]
    across_x = exchange(mine, "group", 2)
    pair = jnp.concatenate([left, output_right], axis=0)
    partner = exchange(pair, "tensor", 1)
    corner = lax.ppermute(pair, ("group", "tensor"), both)
    return mine, across_x, partner, corner


def on_device(
    tokens,
    expert_norm_gain,
    routing,
    chosen_expert_weights,
    resident_gate_weight,
    resident_up_weight,
    resident_down_weight,
    adapter_input_left,
    adapter_input_right,
    adapter_output_left,
    adapter_output_right,
):
    rows, width = tokens.shape
    position = lax.axis_index("tensor")
    place = jnp.stack([lax.axis_index("group"), position % 2]).astype(jnp.int32)
    pieces = gather_factors(
        adapter_input_left, adapter_input_right, adapter_output_left, adapter_output_right
    )
    route_t, gain = routing.T, expert_norm_gain.reshape(1, width)
    sent = [dispatch(tokens, gain, route_t, first) for first in range(0, CAP, PART)]
    mix = mixing(route_t, chosen_expert_weights.T, rows)

    def travel(value):
        value = value.reshape(2 * EXPERTS, PART, width)
        return lax.all_to_all(value, "tensor", 0, 0, tiled=True).reshape(-1, width)

    weights = (resident_gate_weight, resident_up_weight, resident_down_weight)
    arrived = [travel(value) for value in sent]
    *pieces, arrived[0] = lax.optimization_barrier((*pieces, arrived[0]))
    own = stack(pieces)
    far = exchange(own, "group", 1)
    parts = [
        travel(feed_forward(place, x, *weights, own, far, limit))
        for x, limit in zip(arrived, FFN_VMEM)
    ]
    base = combine(mix[0], parts[0], None, F32)
    return combine(mix[1], parts[1], base, BF16)


def solution(mesh):
    return jax.shard_map(
        on_device,
        mesh=mesh,
        in_specs=(
            P(("group", "tensor"), None),
            P(),
            P("group", None),
            P("group", None),
            P(None, "tensor"),
            P(None, "tensor"),
            P("tensor", None),
            P(None, "group", "tensor"),
            P(None, "group", "tensor"),
            P("tensor", "group"),
            P("group", "tensor"),
        ),
        out_specs=P(("group", "tensor"), None),
        check_vma=False,
    )
```

```python
import functools

import jax
import jax.numpy as jnp
from jax import lax
from jax.experimental import pallas as pl
from jax.experimental.pallas import tpu as pltpu
from jax.sharding import PartitionSpec as P

ADAPTER_SCALE = 0.5
NORM_EPS = 1e-06
EXPERTS = 16
CAP = 16
PART = CAP // 2
FFN_VMEM = (50 << 20, 62 << 20)
ROWS_AT = ((0, 128), (64, 176))
DISPATCH_VMEM = 64 << 20
F32 = jnp.float32
BF16 = jnp.bfloat16
NT = (((1,), (1,)), ((), ()))
TN = (((0,), (0,)), ((), ()))


def exchange(value, axis, bit):
    return lax.ppermute(value, axis, [(i, i ^ bit) for i in range(lax.axis_size(axis))])


def own_rows(table_ref, rows):
    position = lax.axis_index("tensor")
    per = 128 // rows
    start = pl.multiple_of((position // per) * 128, 128)
    block = table_ref[:, pl.ds(start, 128)]
    return pltpu.roll(block, (128 - (position % per) * rows) % 128, 1)[:, 0:rows]


def slots_of(route_t, depth, copies, first):
    rows = route_t.shape[1]
    experts = lax.broadcasted_iota(jnp.int32, (EXPERTS, rows), 0)
    chosen = jnp.zeros((EXPERTS, rows), jnp.bool_)
    for k in range(route_t.shape[0]):
        chosen = chosen | (route_t[k : k + 1, :] == experts)
    upper = (
        lax.broadcasted_iota(jnp.int32, (rows, rows), 0)
        <= lax.broadcasted_iota(jnp.int32, (rows, rows), 1)
    ).astype(F32)
    place = jnp.dot(chosen.astype(F32), upper, preferred_element_type=F32).astype(jnp.int32) - 1
    place = jnp.where(chosen, place, -1)
    slot = lax.broadcasted_iota(jnp.int32, (EXPERTS, copies * depth, rows), 1) % depth
    return place[:, None, :] == slot + first


def dispatch_body(first, tokens_ref, gain_ref, route_ref, out_ref, normed_ref, mask_ref):
    step = pl.program_id(0)

    @pl.when(step == 0)
    def _():
        wide = tokens_ref[...].astype(F32)
        spread = jnp.mean(wide * wide, axis=-1, keepdims=True)
        normed_ref[...] = (wide * lax.rsqrt(spread + NORM_EPS) * gain_ref[...]).astype(BF16)
        mask = slots_of(own_rows(route_ref, tokens_ref.shape[0]), PART, 1, first)
        mask_ref[...] = mask.astype(F32).reshape(EXPERTS * PART, -1).astype(BF16)

    per = out_ref.shape[0]
    pick = mask_ref[pl.ds(pl.multiple_of(step * per * PART, per * PART), per * PART), :]
    rows = jnp.dot(pick, normed_ref[...], preferred_element_type=F32)
    rows = rows.reshape(per, 1, PART, rows.shape[1]).astype(BF16)
    out_ref[...] = jnp.broadcast_to(rows, out_ref.shape)


def dispatch(tokens, gain, route_t, first):
    rows, width = tokens.shape
    steps = 2
    per = EXPERTS // steps
    return pl.pallas_call(
        functools.partial(dispatch_body, first),
        grid=(steps,),
        out_shape=pltpu.HBM((EXPERTS, 2, PART, width), BF16),
        in_specs=[
            pl.BlockSpec((rows, width), lambda i: (0, 0)),
            pl.BlockSpec((1, width), lambda i: (0, 0)),
            pl.BlockSpec(route_t.shape, lambda i: (0, 0)),
        ],
        out_specs=pl.BlockSpec((per, 2, PART, width), lambda i: (i, 0, 0, 0)),
        scratch_shapes=[pltpu.VMEM((rows, width), BF16), pltpu.VMEM((EXPERTS * PART, rows), BF16)],
        compiler_params=pltpu.CompilerParams(vmem_limit_bytes=DISPATCH_VMEM),
        cost_estimate=pl.CostEstimate(
            flops=2 * EXPERTS * PART * rows * width, bytes_accessed=3 << 20, transcendentals=0
        ),
        name="dispatch",
    )(tokens, gain, route_t)


def mixing_body(rows, route_ref, weight_ref, out_ref):
    route_t, weight_t = own_rows(route_ref, rows), own_rows(weight_ref, rows)
    experts = lax.broadcasted_iota(jnp.int32, (EXPERTS, rows), 0)
    weight = jnp.zeros((EXPERTS, rows), F32)
    for k in range(route_t.shape[0]):
        weight += jnp.where(route_t[k : k + 1, :] == experts, weight_t[k : k + 1, :], 0.0)
    for part in range(CAP // PART):
        mask = slots_of(route_t, PART, 2, part * PART)
        spread = jnp.where(mask, weight[:, None, :], 0.0).reshape(2 * EXPERTS * PART, rows).T
        high = spread.astype(BF16)
        out_ref[part, 0:rows, :] = high
        out_ref[part, rows : 2 * rows, :] = (spread - high.astype(F32)).astype(BF16)


def mixing(route_t, weight_t, rows):
    vmem = pl.BlockSpec(memory_space=pltpu.VMEM)
    return pl.pallas_call(
        functools.partial(mixing_body, rows),
        in_specs=[vmem, vmem],
        out_specs=vmem,
        out_shape=jax.ShapeDtypeStruct((CAP // PART, 2 * rows, 2 * EXPERTS * PART), BF16),
        cost_estimate=pl.CostEstimate(flops=1 << 20, bytes_accessed=1 << 17, transcendentals=0),
        name="mixing",
    )(route_t, weight_t)


def ffn_body(
    place_ref, x_ref, wg_ref, wu_ref, wd_ref, own_ref, far_ref, out_ref,
    gate_ref, up_ref, low_ref, right_ref, hidden_ref, mid_ref, outr_ref,
):
    step = pl.program_id(0)
    group, half = place_ref[0], place_ref[1]
    width = hidden_ref.shape[1]
    span = x_ref.shape[1]
    packs = (own_ref, far_ref)

    for turn in range(4):

        @pl.when(step == turn)
        def _(turn=turn):
            xh, pack = turn // 2, packs[turn % 2]
            there = group ^ turn
            near, across = ROWS_AT[xh]
            x = x_ref[...]
            left = jnp.concatenate(
                [
                    pack[near : near + 32, 0:span],
                    pack[near : near + 32, span : 2 * span],
                    pack[across : across + 32, 0:span],
                    pack[across : across + 32, span : 2 * span],
                ],
                axis=0,
            )
            gate = jnp.dot(x, wg_ref[...], preferred_element_type=F32)
            up = jnp.dot(x, wu_ref[...], preferred_element_type=F32)
            low = lax.dot_general(x, left, NT, preferred_element_type=F32)
            if turn == 0:
                right_ref[...] = jnp.zeros_like(right_ref)
            else:
                gate += gate_ref[...]
                up += up_ref[...]
                low += low_ref[...]
            ranks = (half ^ (there >> 1)) * 64 + (there & 1) * 16
            r0 = pl.multiple_of(ranks, 16)
            r1 = pl.multiple_of(ranks + 32, 16)
            right_ref[pl.ds(r0, 16), 0:width] = pack[near + 48 : near + 64, 0:width]
            right_ref[pl.ds(r1, 16), width : 2 * width] = pack[
                near + 48 : near + 64, width : 2 * width
            ]
            cols = outr_ref.shape[2]
            outr_ref[0, turn * 16 : turn * 16 + 16, :] = pack[near + 32 : near + 48, 0:cols]
            outr_ref[1, turn * 16 : turn * 16 + 16, :] = pack[across + 32 : across + 48, 0:cols]
            if turn < 3:
                gate_ref[...], up_ref[...], low_ref[...] = gate, up, low
                return
            scaled = (ADAPTER_SCALE * low).astype(BF16)
            gate += jnp.dot(scaled, right_ref[:, 0:width], preferred_element_type=F32)
            up += jnp.dot(scaled, right_ref[:, width : 2 * width], preferred_element_type=F32)
            hidden = (jax.nn.silu(gate) * up).astype(BF16)
            hidden_ref[...] = hidden
            left = jnp.concatenate(
                [
                    packs[t % 2][
                        ROWS_AT[t // 2][0] + 48 : ROWS_AT[t // 2][0] + 64, 2 * width : 3 * width
                    ]
                    for t in range(4)
                ],
                axis=0,
            )
            mid = lax.dot_general(hidden, left, NT, preferred_element_type=F32)
            mid_ref[...] = (ADAPTER_SCALE * mid).astype(BF16)

    @pl.when(step >= 4)
    def _():
        cols = out_ref.shape[1]
        start = (step - 4) * cols
        side = start // outr_ref.shape[2]
        offset = pl.multiple_of(start - side * outr_ref.shape[2], cols)
        out = jnp.dot(hidden_ref[...], wd_ref[...], preferred_element_type=F32)
        out += jnp.dot(
            mid_ref[...], outr_ref[half ^ side, :, pl.ds(offset, cols)], preferred_element_type=F32
        )
        out_ref[...] = out.astype(BF16)


def feed_forward(place, x, wg, wu, wd, own, far, limit):
    rows, width = x.shape
    hidden = wg.shape[1]
    span, cols = width // 4, 2048
    turn = lambda i, s: s[0] ^ jnp.minimum(i, 3)
    later = lambda i: jnp.maximum(i - 4, 0)
    whole = lambda a: pl.BlockSpec(a.shape, lambda i, s: (0,) * a.ndim)
    return pl.pallas_call(
        ffn_body,
        grid_spec=pltpu.PrefetchScalarGridSpec(
            num_scalar_prefetch=1,
            grid=(4 + width // cols,),
            in_specs=[
                pl.BlockSpec((rows, span), lambda i, s: (0, turn(i, s))),
                pl.BlockSpec((span, hidden), lambda i, s: (turn(i, s), 0)),
                pl.BlockSpec((span, hidden), lambda i, s: (turn(i, s), 0)),
                pl.BlockSpec((hidden, cols), lambda i, s: (0, later(i))),
                whole(own),
                whole(far),
            ],
            out_specs=pl.BlockSpec((rows, cols), lambda i, s: (0, later(i))),
            scratch_shapes=[
                pltpu.VMEM((rows, hidden), F32),
                pltpu.VMEM((rows, hidden), F32),
                pltpu.VMEM((rows, 128), F32),
                pltpu.VMEM((128, 2 * hidden), BF16),
                pltpu.VMEM((rows, hidden), BF16),
                pltpu.VMEM((rows, 64), BF16),
                pltpu.VMEM((2, 64, width // 2), BF16),
            ],
        ),
        out_shape=pltpu.HBM((rows, width), BF16),
        compiler_params=pltpu.CompilerParams(vmem_limit_bytes=limit),
        cost_estimate=pl.CostEstimate(
            flops=6 * rows * width * hidden, bytes_accessed=28 << 20, transcendentals=rows * hidden
        ),
        name="feed_forward",
    )(place, x, wg, wu, wd, own, far)


def combine_body(mix_ref, part_ref, *refs):
    out_ref = refs[-1]
    rows = out_ref.shape[0]
    both = jnp.dot(mix_ref[...], part_ref[...], preferred_element_type=F32)
    total = both[0:rows] + both[rows : 2 * rows]
    if len(refs) == 2:
        total += refs[0][...]
    out_ref[...] = total.astype(out_ref.dtype)


def combine(mix, which, part, base, out_type):
    slots, width = part.shape
    rows = mix.shape[1] // 2
    cols = width
    sheet = pl.BlockSpec((rows, cols), lambda i: (0, i))
    in_specs = [
        pl.BlockSpec((None, *mix.shape[1:]), lambda i: (which, 0, 0)),
        pl.BlockSpec((slots, cols), lambda i: (0, i)),
    ]
    operands = (mix, part)
    if base is not None:
        in_specs.append(sheet)
        operands += (base,)
    return pl.pallas_call(
        combine_body,
        grid=(width // cols,),
        out_shape=jax.ShapeDtypeStruct((rows, width), out_type),
        in_specs=in_specs,
        out_specs=sheet,
        compiler_params=pltpu.CompilerParams(vmem_limit_bytes=32 << 20),
        cost_estimate=pl.CostEstimate(
            flops=4 * slots * rows * width, bytes_accessed=3 << 20, transcendentals=0
        ),
        name="combine",
    )(*operands)


def stack(pieces):
    rows, total, at = sum(piece.shape[0] for piece in pieces), None, 0
    wide = max(piece.shape[1] for piece in pieces)
    for piece in pieces:
        after = rows - at - piece.shape[0]
        padded = jnp.pad(piece, ((at, after), (0, wide - piece.shape[1])))
        total = padded if total is None else total + padded
        at += piece.shape[0]
    return total


def gather_factors(input_left, input_right, output_left, output_right):
    left = jnp.transpose(input_left, (2, 0, 1)).reshape(input_left.shape[2], -1)
    right = jnp.concatenate([input_right[0], input_right[1], output_left.T], axis=1)
    wide = right.shape[1]
    pad = lambda a: jnp.pad(a, ((0, 0), (0, wide - a.shape[1])))
    mine = jnp.concatenate([pad(left), pad(output_right), right], axis=0)
    groups, tensor = lax.axis_size("group"), lax.axis_size("tensor")
    both = [
        (g * tensor + t, (g ^ 2) * tensor + (t ^ 1)) for g in range(groups) for t in range(tensor)
    ]
    across_x = exchange(mine, "group", 2)
    pair = jnp.concatenate([left, output_right], axis=0)
    partner = exchange(pair, "tensor", 1)
    corner = lax.ppermute(pair, ("group", "tensor"), both)
    return mine, across_x, partner, corner


def on_device(
    tokens,
    expert_norm_gain,
    routing,
    chosen_expert_weights,
    resident_gate_weight,
    resident_up_weight,
    resident_down_weight,
    adapter_input_left,
    adapter_input_right,
    adapter_output_left,
    adapter_output_right,
):
    rows, width = tokens.shape
    position = lax.axis_index("tensor")
    place = jnp.stack([lax.axis_index("group"), position % 2]).astype(jnp.int32)
    pieces = gather_factors(
        adapter_input_left, adapter_input_right, adapter_output_left, adapter_output_right
    )
    route_t, gain = routing.T, expert_norm_gain.reshape(1, width)
    sent = [dispatch(tokens, gain, route_t, first) for first in range(0, CAP, PART)]
    mix = mixing(route_t, chosen_expert_weights.T, rows)

    def travel(value):
        value = value.reshape(2 * EXPERTS, PART, width)
        return lax.all_to_all(value, "tensor", 0, 0, tiled=True).reshape(-1, width)

    weights = (resident_gate_weight, resident_up_weight, resident_down_weight)
    arrived = [travel(value) for value in sent]
    *pieces, arrived[0] = lax.optimization_barrier((*pieces, arrived[0]))
    own = stack(pieces)
    far = exchange(own, "group", 1)
    parts = [
        travel(feed_forward(place, x, *weights, own, far, limit))
        for x, limit in zip(arrived, FFN_VMEM)
    ]
    base = combine(mix, 0, parts[0], None, F32)
    return combine(mix, 1, parts[1], base, BF16)


def solution(mesh):
    return jax.shard_map(
        on_device,
        mesh=mesh,
        in_specs=(
            P(("group", "tensor"), None),
            P(),
            P("group", None),
            P("group", None),
            P(None, "tensor"),
            P(None, "tensor"),
            P("tensor", None),
            P(None, "group", "tensor"),
            P(None, "group", "tensor"),
            P("tensor", "group"),
            P("group", "tensor"),
        ),
        out_specs=P(("group", "tensor"), None),
        check_vma=False,
    )
```
